256 devices in a mesh: pair: 64 (over z_lo, x, y, core), chol: 4 (over z_hi).
Axes of the slice: x: 4, y: 4, z: 8 (z_hi: 4, z_lo: 2; z = z_hi * 2 + z_lo), core: 2. Of those that a mesh axis runs over, the one named last changes fastest.
Arguments:
- chol_ov: float32 [2048, 64, 768], P('chol', 'pair'), may hold values from -0.5 to 0.5
- chol_oo: float32 [2048, 64, 64], P('chol', 'pair'), may hold values from -0.5 to 0.5
- amplitudes: float32 [2, 64, 768], P(None, 'pair'), may hold values from -0.6 to 0.6
- eps_occ: float32 [64], P('pair'), may hold values from -2.5 to -0.4
- eps_vir: float32 [768], replicated, may hold values from 0.3 to 3
- fock: float32 [64, 768], P('pair'), may hold values from -0.3 to 0.3
Outputs:
- omega: float32 [2, 2, 768], replicated
The draws below stay inside these ranges and needn't reach their ends.
All inputs are finite; a program needn't handle non-finite values.
Results may differ from the reference program's by a relative error of at most 0.00011.
Values sent between devices are 32-bit elements; how exact they have to be, the bound alone decides.
A program may use at most 64 MiB of HBM per device.

```python
import jax
import jax.numpy as jnp
from jax import lax

V = 768
NQ = 2048
WIN = 2
O = 64


def shard_levels(own_key, shape, cuts, least, high):
    def one(axis_at, parts):
        heights = jax.random.uniform(jax.random.fold_in(jax.random.fold_in(own_key, 6), axis_at), (parts,), jnp.float32, least / len(cuts), high / len(cuts))
        return jnp.repeat(jnp.exp(heights), shape[axis_at] // parts).reshape((-1,) + (1,) * (len(shape) - axis_at - 1))

    gain = one(*cuts[0])
    for cut in cuts[1:]:
        gain = gain * one(*cut)
    return gain


def scatter_about(own_key, dims, deviation, bound, cuts=(), kind=jnp.bfloat16):
    drawn = deviation * jax.random.normal(own_key, dims, jnp.float32)
    if cuts:
        drawn = drawn * shard_levels(own_key, dims, cuts, -0.22, 0.18)
    return jnp.clip(drawn, -bound, bound).astype(kind)


def setup_inputs(seed: int = 0) -> dict:
    key_list = jax.random.split(jax.random.key(seed), 7)
    chol_ov = scatter_about(key_list[0], (NQ, O, V), 0.08, 0.5, ((0, 4), (1, 64)), jnp.float32)
    chol_oo = scatter_about(key_list[1], (NQ, O, O), 0.08, 0.5, ((0, 4), (1, 64)), jnp.float32)
    amplitudes = scatter_about(key_list[2], (2, O, V), 0.1, 0.6, ((1, 64),), jnp.float32)
    eps_occ = jnp.clip(-2.5 + 2.1 * jax.random.uniform(key_list[3], (O,), jnp.float32) ** shard_levels(key_list[3], (O,), ((0, 64),), -0.2, 0.2), -2.5, -0.4)
    eps_vir = jnp.clip(jax.random.uniform(key_list[4], (V,), jnp.float32, 0.3, 3.0), 0.3, 3.0)
    fock = scatter_about(key_list[5], (O, V), 0.05, 0.3, ((0, 64),), jnp.float32)
    return dict(chol_ov=chol_ov, chol_oo=chol_oo, amplitudes=amplitudes, eps_occ=eps_occ, eps_vir=eps_vir, fock=fock)


STEP_TIME = 0.7


def dress_all(chol_ov, chol_oo, amplitudes):
    count_q, count_o, count_v = chol_ov.shape
    flat = chol_oo.reshape(count_q * count_o, chol_oo.shape[2])
    real_part = chol_ov - jnp.dot(flat, amplitudes[0], precision=lax.Precision.HIGHEST).reshape(count_q, count_o, count_v)
    imag_part = -jnp.dot(flat, amplitudes[1], precision=lax.Precision.HIGHEST).reshape(count_q, count_o, count_v)
    return real_part, imag_part


def reference(chol_ov, chol_oo, amplitudes, eps_occ, eps_vir, fock):
    hi = lax.Precision.HIGHEST
    dressed_r, dressed_i = dress_all(chol_ov, chol_oo, amplitudes)
    count_o = chol_ov.shape[1]
    count_v = chol_ov.shape[2]
    real_rows = []
    imag_rows = []
    for window in range(WIN):
        left_r = dressed_r[:, window, :]
        left_i = dressed_i[:, window, :]
        e_left = eps_occ[window]

        def add_pair(total, j):
            right_r = lax.dynamic_index_in_dim(dressed_r, j, 1, keepdims=False)
            right_i = lax.dynamic_index_in_dim(dressed_i, j, 1, keepdims=False)
            g_real = jnp.dot(left_r.T, right_r, precision=hi) - jnp.dot(left_i.T, right_i, precision=hi)
            g_imag = jnp.dot(left_r.T, right_i, precision=hi) + jnp.dot(left_i.T, right_r, precision=hi)
            e_right = lax.dynamic_index_in_dim(eps_occ, j, 0, keepdims=False)
            denom = eps_vir[:, None] + eps_vir[None, :] - e_left - e_right
            w_real = (1.0 - jnp.cos(STEP_TIME * denom)) / denom
            w_imag = jnp.sin(STEP_TIME * denom) / denom
            t_real = w_real * g_real - w_imag * g_imag
            t_imag = w_real * g_imag + w_imag * g_real
            fock_row = lax.dynamic_index_in_dim(fock, j, 0, keepdims=False)
            o_real = 2.0 * jnp.dot(t_real, fock_row, precision=hi) - jnp.dot(fock_row, t_real, precision=hi)
            o_imag = 2.0 * jnp.dot(t_imag, fock_row, precision=hi) - jnp.dot(fock_row, t_imag, precision=hi)
            return total + jnp.stack([o_real, o_imag]), None

        start = jnp.zeros((2, count_v), jnp.float32)
        total, unused = lax.scan(add_pair, start, jnp.arange(count_o, dtype=jnp.int32))
        real_rows.append(total[0])
        imag_rows.append(total[1])
    return jnp.stack([jnp.stack(real_rows), jnp.stack(imag_rows)])
```

```python
import math

import jax
import jax.numpy as jnp
from jax import lax
from jax.experimental import pallas as pl
from jax.experimental.pallas import tpu as pltpu
from jax.sharding import PartitionSpec as P

WIN = 2
STEP_TIME = 0.7
HALF = STEP_TIME / 2
RANK = 8
VIR_LOW, VIR_HIGH = 0.3, 3.0
OCC_LOW, OCC_HIGH = -2.5, -0.4
PAIR, CHOL = 64, 4
SLOTS = PAIR // 2
PLANE = 16
LINE = 8
V, NQ, O = 768, 512, 64
ROW = 2 * V + 128
MESH = pl.DeviceIdType.MESH
F32 = jnp.float32
BF16 = jnp.bfloat16
NN = (((1,), (0,)), ((), ()))
NT = (((1,), (1,)), ((), ()))


def nodes_on(low, high):
    mid, half = (low + high) / 2, (high - low) / 2
    return [mid + half * math.cos((2 * m + 1) * math.pi / (2 * RANK)) for m in range(RANK)]


VIR_NODES = nodes_on(VIR_LOW, VIR_HIGH)
PAIR_NODES = nodes_on(VIR_LOW - OCC_HIGH, VIR_HIGH - OCC_LOW)
PAIR_MID = (VIR_LOW - OCC_HIGH + VIR_HIGH - OCC_LOW) / 2


def by_row(values, width):
    row = lax.broadcasted_iota(jnp.int32, (RANK, width), 0)
    out = jnp.full((RANK, width), values[0], F32)
    for m in range(1, RANK):
        out = jnp.where(row == m, F32(values[m]), out)
    return out


def basis(nodes, at):
    scale = []
    for m in range(RANK):
        den = 1.0
        for n in range(RANK):
            if n != m:
                den *= nodes[m] - nodes[n]
        scale.append(1.0 / den)
    width = at.shape[1]
    row = lax.broadcasted_iota(jnp.int32, (RANK, width), 0)
    out = by_row(scale, width)
    for n in range(RANK):
        out = out * jnp.where(row == n, F32(1.0), at - F32(nodes[n]))
    return out


def weight(denom):
    s, c = jnp.sin(HALF * denom), jnp.cos(HALF * denom)
    q = 2.0 * s / denom
    return q * s, q * c


def split(x):
    hi = x.astype(BF16)
    return hi, (x - hi.astype(F32)).astype(BF16)


def dot(a, b, dims):
    return lax.dot_general(a, b, dims, preferred_element_type=F32)


def dot3(a, b, dims):
    a_hi, a_lo = a
    b_hi, b_lo = b
    rows = a_hi.shape[0]
    both = dot(jnp.concatenate([a_hi, a_lo], axis=0), b_hi, dims)
    return both[:rows] + both[rows:] + dot(a_hi, b_lo, dims)


def kernel(
    ov, oo, amps, eocc, evir, fock, out,
    l_hi, l_lo, l_other, t_all, f_all, fm_hi, fm_lo, z_out, z_in, oo_out, oo_all,
    x_own, x_in, x_sum, x_all, x_fin, om, om_in, om_pl, om_ln, om_fin,
    t_snd, t_rcv, tp_snd, tp_rcv, f_snd, f_rcv, l_snd, l_rcv, z_snd, z_rcv,
    o_snd, o_rcv, oa_snd, oa_rcv, op_snd, op_rcv, xp_snd, xp_rcv, xr_snd, xr_rcv, xs_snd, xs_rcv,
    r1_snd, r1_rcv, r2_snd, r2_rcv, r3_snd, r3_rcv, r4_snd, r4_rcv,
):
    p, c = lax.axis_index("pair"), lax.axis_index("chol")
    core = lax.rem(p, 2)
    slot = p // 2
    peer = p + 1 - 2 * core
    plane = lax.rem(slot, PLANE)
    z_lo = p // (PAIR // 2)
    line = 2 * c + z_lo

    def copy(src, dst, snd, rcv, pair, chol):
        return pltpu.make_async_remote_copy(
            src_ref=src, dst_ref=dst, send_sem=snd, recv_sem=rcv,
            device_id=(pair, chol), device_id_type=MESH,
        )

    def local(ref, sem):
        return pltpu.make_async_copy(ref, ref, sem)

    def mate(k):
        return lax.rem(p + 2 * k, PAIR)

    def line_mate(k):
        z = lax.rem(line + k, LINE)
        return lax.rem(p, PAIR // 2) + (PAIR // 2) * lax.rem(z, 2), z // 2

    barrier = pltpu.get_barrier_semaphore()
    pl.semaphore_signal(barrier, inc=1, device_id=(peer, c), device_id_type=MESH)

    @pl.loop(1, SLOTS)
    def _(k):
        pl.semaphore_signal(barrier, inc=1, device_id=(mate(k), c), device_id_type=MESH)

    for k in range(1, LINE):
        @pl.when(lax.rem(line + k, LINE) // 2 != c)
        def _(k=k):
            pair, chol = line_mate(k)
            pl.semaphore_signal(barrier, inc=1, device_id=(pair, chol), device_id_type=MESH)

    e_vir = evir[...]
    e_own = eocc[...]
    f_row = fock[...]
    t_all[slot, core, :, 0:V] = amps[0:1, :]
    t_all[slot, core, :, V:2 * V] = amps[1:2, :]
    t_all[slot, core, :, 2 * V:ROW] = jnp.broadcast_to(e_own, (1, 128))

    @pl.when(slot == 0)
    def _():
        oo_t = jnp.transpose(oo[...])
        for k in range(SLOTS):
            oo_out[k] = oo_t[8 * (k // 4):8 * (k // 4) + 8, 128 * (k % 4):128 * (k % 4) + 128]

    poly = basis(VIR_NODES, jnp.broadcast_to(e_vir, (RANK, V)))
    gap = jnp.broadcast_to(e_vir - e_own, (RANK, V))
    turn = HALF * (gap - PAIR_MID)
    pair_poly = basis(PAIR_NODES, gap) * f_row
    f_vir = poly * f_row
    f_pair = jnp.concatenate([pair_poly * jnp.cos(turn), -pair_poly * jnp.sin(turn)], axis=0)
    hi, lo = split(ov[...])
    l_hi[...] = hi
    l_lo[...] = lo

    pl.semaphore_wait(barrier, 1 + (SLOTS - 1) + (LINE - 2))

    fock_copy = copy(fock, f_all.at[slot], f_snd, f_rcv, core, c)

    @pl.when(slot != 0)
    def _():
        fock_copy.start()

    slab_copy = copy(ov, l_other, l_snd, l_rcv, peer, c)

    @pl.when(slot == 0)
    def _():
        slab_copy.start()

        @pl.loop(1, SLOTS)
        def _(k):
            copy(oo_out.at[k], oo_all.at[core, pl.ds(pl.multiple_of(8 * (k // 4), 8), 8), pl.ds(pl.multiple_of(128 * lax.rem(k, 4), 128), 128)],
                 o_snd, o_rcv, 2 * k + core, c).start()

        oo_all[core, 0:8, 0:128] = oo_out[0]
        f_all[0] = fock[...]

    @pl.loop(1, SLOTS)
    def _(k):
        row = t_all.at[slot, core]
        copy(row, row, t_snd, t_rcv, mate(k), c).start()

    oo_mine = oo_all.at[core, pl.ds(pl.multiple_of(8 * (slot // 4), 8), 8), pl.ds(pl.multiple_of(128 * lax.rem(slot, 4), 128), 128)]

    def pass_on():
        @pl.loop(1, SLOTS)
        def _(k):
            copy(oo_mine, oo_mine, oa_snd, oa_rcv, mate(k), c).start()

    @pl.when(slot == 0)
    def _():
        pass_on()
        local(f_all.at[pl.ds(1, SLOTS - 1)], f_rcv).wait()
        for k in range(0, SLOTS, 2):
            pairs = jnp.concatenate([poly * f_all[k], poly * f_all[k + 1]], axis=0)
            hi, lo = split(pairs)
            fm_hi[8 * k:8 * k + 16, :] = hi
            fm_lo[8 * k:8 * k + 16, :] = lo

        def project(window, b_hi, b_lo):
            z = dot3((fm_hi[...], fm_lo[...]), (b_hi, b_lo), NT)
            for k in range(SLOTS):
                z_out[window, k] = z[8 * k:8 * k + 8, :]

            @pl.loop(1, SLOTS)
            def _(k):
                copy(z_out.at[window, k], z_in.at[window], z_snd.at[window], z_rcv.at[window], 2 * k + core, c).start()

            z_in[window] = z_out[window, 0]

        project(core, l_hi[...], l_lo[...])
        slab_copy.wait_recv()
        hi, lo = split(l_other[...])
        project(1 - core, hi, lo)

    @pl.when(slot != 0)
    def _():
        local(oo_mine, o_rcv).wait()
        pass_on()

    local(t_all.at[pl.ds(0, SLOTS - 1), core], t_rcv).wait()
    rows = t_all.at[:, core]
    t_swap = copy(rows, rows, tp_snd, tp_rcv, peer, c)
    t_swap.start()
    x_left = dot3(split(f_pair), (l_hi[...], l_lo[...]), NT)
    other_rows = t_all.at[:, 1 - core]
    copy(other_rows, other_rows, tp_snd, tp_rcv, peer, c).wait_recv()
    t_re = split(t_all[:, :, 0, 0:V].reshape(O, V))
    t_im = split(t_all[:, :, 0, V:2 * V].reshape(O, V))
    lhs = split(jnp.concatenate([f_vir, f_pair], axis=0))
    tf_re, tf_im = dot3(lhs, t_re, NT), dot3(lhs, t_im, NT)
    oo_own = split(oo[...])
    tx = jnp.concatenate([tf_re[8:16] - tf_im[16:24], tf_im[8:16] + tf_re[16:24]], axis=0)
    x_terms = x_left - dot3(split(tx), oo_own, NT)
    x_own[0] = x_terms[0:8]
    x_own[1] = x_terms[8:16]
    x_swap = copy(x_own.at[1 - core], x_in, xp_snd, xp_rcv, peer, c)
    x_swap.start()
    x_swap.wait_recv()
    x_sum[...] = x_own[core] + x_in[...]
    x_copy = copy(x_sum, x_all.at[slot], xr_snd, xr_rcv, core, c)

    @pl.when(slot != 0)
    def _():
        x_copy.start()

    local(oo_out.at[pl.ds(0, SLOTS - 1)], oa_rcv).wait()
    oo_swap = copy(oo_all.at[core], oo_all.at[core], op_snd, op_rcv, peer, c)
    oo_swap.start()
    copy(oo_all.at[1 - core], oo_all.at[1 - core], op_snd, op_rcv, peer, c).wait_recv()
    tz = split(jnp.concatenate([tf_re[0:8], tf_im[0:8]], axis=0))
    dress = [dot3(tz, split(oo_all[i]), NN) for i in range(WIN)]

    def through(ct):
        ct = split(ct)
        lv = dot3(ct, (l_hi[...], l_lo[...]), NN)
        r = split(dot3(ct, oo_own, NN))
        rt_re, rt_im = dot3(r, t_re, NN), dot3(r, t_im, NN)
        parts = []
        for g in range(0, lv.shape[0], 16):
            re, im = slice(g, g + 8), slice(g + 8, g + 16)
            parts.append((
                lv[re] - (rt_re[re] - rt_im[im]),
                lv[im] - (rt_im[re] + rt_re[im]),
            ))
        return parts

    def fold(w_re, w_im, v_re, v_im):
        re = jnp.sum(w_re * v_re - w_im * v_im, axis=0, keepdims=True)
        im = jnp.sum(w_re * v_im + w_im * v_re, axis=0, keepdims=True)
        return re, im

    e_win = [t_all[0, i, :, 2 * V:2 * V + 1] for i in range(WIN)]

    @pl.when(slot != 0)
    def _():
        for i in range(WIN):
            local(z_in.at[i], z_rcv.at[i]).wait()

    cols = []
    for i in range(WIN):
        cols += [z_in[i] - dress[i][0:8], -dress[i][8:16]]
    vir_rows = by_row(VIR_NODES, V)
    for i, (v_re, v_im) in enumerate(through(jnp.concatenate(cols, axis=0))):
        w_re, w_im = weight(e_vir + vir_rows - (e_win[i] + e_own))
        re, im = fold(w_re, w_im, v_re, v_im)
        om[i, :, 0:V] = -re
        om[i, :, V:2 * V] = -im

    @pl.when(slot == 0)
    def _():
        x_all[0] = x_sum[...]
        local(x_all.at[pl.ds(1, SLOTS - 1)], xr_rcv).wait()
        total = x_all[0]
        for k in range(1, SLOTS):
            total = total + x_all[k]
        x_fin[core] = total
        swap = copy(x_fin.at[core], x_fin.at[core], xs_snd, xs_rcv, peer, c)
        swap.start()
        copy(x_fin.at[1 - core], x_fin.at[1 - core], xs_snd, xs_rcv, peer, c).wait_recv()
        (v_re, v_im), = through(jnp.concatenate([x_fin[0], x_fin[1]], axis=0))
        w_re, w_im = weight(e_vir + by_row(PAIR_NODES, V) - e_own)
        turns = [HALF * (g - PAIR_MID) for g in PAIR_NODES]
        t_cos = by_row([math.cos(g) for g in turns], V)
        t_sin = by_row([math.sin(g) for g in turns], V)
        re, im = fold(w_re * t_cos - w_im * t_sin, w_re * t_sin + w_im * t_cos, v_re, v_im)
        om[core, :, 0:V] += 2.0 * re
        om[core, :, V:2 * V] += 2.0 * im
        swap.wait_send()

    first = copy(om.at[1 - core], om_in, r1_snd, r1_rcv, peer, c)
    first.start()
    first.wait_recv()
    om_pl[plane] = om[core] + om_in[...]

    @pl.loop(1, PLANE)
    def _(k):
        to = (PAIR // 2) * z_lo + lax.rem(lax.rem(p, PAIR // 2) + 2 * k, PAIR // 2)
        copy(om_pl.at[plane], om_pl.at[plane], r2_snd, r2_rcv, to, c).start()

    local(om_pl.at[pl.ds(0, PLANE - 1)], r2_rcv).wait()
    total = om_pl[0]
    for k in range(1, PLANE):
        total = total + om_pl[k]
    om_ln[line] = total
    for k in range(1, LINE):
        pair, chol = line_mate(k)
        copy(om_ln.at[line], om_ln.at[line], r3_snd, r3_rcv, pair, chol).start()
    local(om_ln.at[pl.ds(0, LINE - 1)], r3_rcv).wait()
    total = om_ln[0]
    for k in range(1, LINE):
        total = total + om_ln[k]
    om_fin[core] = total
    last = copy(om_fin.at[core], om_fin.at[core], r4_snd, r4_rcv, peer, c)
    last.start()
    copy(om_fin.at[1 - core], om_fin.at[1 - core], r4_snd, r4_rcv, peer, c).wait_recv()
    for i in range(WIN):
        for r in range(2):
            out[r, i:i + 1, :] = om_fin[i, :, r * V:(r + 1) * V]

    last.wait_send()
    local(om_ln.at[pl.ds(0, LINE - 1)], r3_snd).wait()
    local(om_pl.at[pl.ds(0, PLANE - 1)], r2_snd).wait()
    first.wait_send()
    oo_swap.wait_send()
    x_swap.wait_send()
    t_swap.wait_send()
    local(oo_out.at[pl.ds(0, SLOTS - 1)], oa_snd).wait()
    local(t_all.at[pl.ds(0, SLOTS - 1), core], t_snd).wait()

    @pl.when(slot != 0)
    def _():
        fock_copy.wait_send()
        x_copy.wait_send()

    @pl.when(slot == 0)
    def _():
        slab_copy.wait_send()
        local(oo_out.at[pl.ds(0, SLOTS - 1)], o_snd).wait()
        for i in range(WIN):
            local(z_out.at[i, pl.ds(0, SLOTS - 1)], z_snd.at[i]).wait()


def per_device(chol_ov, chol_oo, amplitudes, eps_occ, eps_vir, fock):
    vmem = pl.BlockSpec(memory_space=pltpu.VMEM)
    dma = pltpu.SemaphoreType.DMA
    scratch = [
        pltpu.VMEM((NQ, V), BF16), pltpu.VMEM((NQ, V), BF16), pltpu.VMEM((NQ, V), F32),
        pltpu.VMEM((SLOTS, 2, 1, ROW), F32), pltpu.VMEM((SLOTS, 1, V), F32),
        pltpu.VMEM((SLOTS * RANK, V), BF16), pltpu.VMEM((SLOTS * RANK, V), BF16),
        pltpu.VMEM((WIN, SLOTS, RANK, NQ), F32), pltpu.VMEM((WIN, RANK, NQ), F32),
        pltpu.VMEM((SLOTS, 8, 128), F32), pltpu.VMEM((WIN, O, NQ), F32),
        pltpu.VMEM((2, RANK, NQ), F32), pltpu.VMEM((RANK, NQ), F32), pltpu.VMEM((RANK, NQ), F32),
        pltpu.VMEM((SLOTS, RANK, NQ), F32), pltpu.VMEM((2, RANK, NQ), F32),
        pltpu.VMEM((WIN, 1, 2 * V), F32), pltpu.VMEM((1, 2 * V), F32),
        pltpu.VMEM((PLANE, 1, 2 * V), F32), pltpu.VMEM((LINE, 1, 2 * V), F32),
        pltpu.VMEM((WIN, 1, 2 * V), F32),
    ]
    sems = [dma] * 8 + [dma((WIN,))] * 2 + [dma] * 20
    return pl.pallas_call(
        kernel,
        out_shape=jax.ShapeDtypeStruct((2, WIN, V), F32),
        in_specs=[vmem] * 6,
        out_specs=vmem,
        scratch_shapes=scratch + sems,
        compiler_params=pltpu.CompilerParams(
            collective_id=0, has_side_effects=True, vmem_limit_bytes=40 * 2**20
        ),
    )(
        chol_ov.reshape(NQ, V), chol_oo.reshape(NQ, O), amplitudes.reshape(2, V),
        eps_occ.reshape(1, 1), eps_vir.reshape(1, V), fock.reshape(1, V),
    )


def solution(mesh):
    return jax.shard_map(
        per_device,
        mesh=mesh,
        in_specs=(
            P("chol", "pair", None),
            P("chol", "pair", None),
            P(None, "pair", None),
            P("pair"),
            P(),
            P("pair", None),
        ),
        out_specs=P(),
        check_vma=False,
    )
```

```python
import math

import jax
import jax.numpy as jnp
from jax import lax
from jax.experimental import pallas as pl
from jax.experimental.pallas import tpu as pltpu
from jax.sharding import PartitionSpec as P

WIN = 2
STEP_TIME = 0.7
HALF = STEP_TIME / 2
RANK = 8
VIR_LOW, VIR_HIGH = 0.3, 3.0
OCC_LOW, OCC_HIGH = -2.5, -0.4
PAIR, CHOL = 64, 4
SLOTS = PAIR // 2
PLANE = 16
LINE = 8
V, NQ, O = 768, 512, 64
LANES = 128
VB = V // LANES
QUARTERS = NQ // LANES
UNIT = LANES * VB
EPS_AT, SENT, MSG = 2 * VB, 2 * VB + 1, 16
MESH = pl.DeviceIdType.MESH
F32 = jnp.float32
BF16 = jnp.bfloat16
NN = (((1,), (0,)), ((), ()))
NT = (((1,), (1,)), ((), ()))


def nodes_on(low, high):
    mid, half = (low + high) / 2, (high - low) / 2
    return [mid + half * math.cos((2 * m + 1) * math.pi / (2 * RANK)) for m in range(RANK)]


VIR_NODES = nodes_on(VIR_LOW, VIR_HIGH)
PAIR_NODES = nodes_on(VIR_LOW - OCC_HIGH, VIR_HIGH - OCC_LOW)
PAIR_MID = (VIR_LOW - OCC_HIGH + VIR_HIGH - OCC_LOW) / 2


def by_row(values, width):
    row = lax.broadcasted_iota(jnp.int32, (RANK, width), 0)
    out = jnp.full((RANK, width), values[0], F32)
    for m in range(1, RANK):
        out = jnp.where(row == m, F32(values[m]), out)
    return out


def basis(nodes, at):
    scale = []
    for m in range(RANK):
        den = 1.0
        for n in range(RANK):
            if n != m:
                den *= nodes[m] - nodes[n]
        scale.append(1.0 / den)
    width = at.shape[1]
    row = lax.broadcasted_iota(jnp.int32, (RANK, width), 0)
    out = by_row(scale, width)
    for n in range(RANK):
        out = out * jnp.where(row == n, F32(1.0), at - F32(nodes[n]))
    return out


def weight(denom):
    s, c = jnp.sin(HALF * denom), jnp.cos(HALF * denom)
    q = 2.0 * s / denom
    return q * s, q * c


def fold(w, v):
    re = jnp.sum(w[0] * v[0] - w[1] * v[1], axis=0, keepdims=True)
    im = jnp.sum(w[0] * v[1] + w[1] * v[0], axis=0, keepdims=True)
    return re, im


def split(x):
    hi = x.astype(BF16)
    return hi, (x - hi.astype(F32)).astype(BF16)


def dot(a, b, dims):
    return lax.dot_general(a, b, dims, preferred_element_type=F32)


def dot3(a, b, dims):
    a_hi, a_lo = a
    b_hi, b_lo = b
    rows = a_hi.shape[0]
    both = dot(jnp.concatenate([a_hi, a_lo], axis=0), b_hi, dims)
    return both[:rows] + both[rows:] + dot(a_hi, b_lo, dims)


def far_first(v):
    return 2 + v - (v // 2) * (2 * v - 1)


def kernel(
    ov, oo, amps, eocc, evir, fock, out,
    raw, oo_in, amps_in, e_in, ev_in, f_in, in_sem,
    oo_q, oo_p, oo_hi, oo_lo, l_hi, l_lo, x_left, msg,
    f_rows, l_other, lx_hi, lx_lo, oo_g, fm_hi, fm_lo, rhs_hi, rhs_lo, z_out, z_in,
    x_out, x_in, x_sum, x_all, x_tot, om, om_in, om_pl, om_ln, om_fin,
    z_snd, z_rcv, l_snd, l_rcv, f_snd, f_rcv, x_snd, x_rcv, xs_snd, xs_rcv, t_snd, t_rcv, tp_snd, tp_rcv,
    oc_snd, oc_rcv, oa_snd, oa_rcv, op_snd, op_rcv, xp_snd, xp_rcv, r1_snd, r1_rcv, r2_snd, r2_rcv, r3_snd, r3_rcv, r4_snd, r4_rcv,
):
    p, c = lax.axis_index("pair"), lax.axis_index("chol")
    core = lax.rem(p, 2)
    slot = p // 2
    peer = p + 1 - 2 * core
    z_lo, x_at, y_at = slot // PLANE, lax.rem(slot // 4, 4), lax.rem(slot, 4)
    plane = lax.rem(slot, PLANE)
    line = 2 * c + z_lo

    def copy(src, dst, snd, rcv, pair, chol):
        return pltpu.make_async_remote_copy(
            src_ref=src, dst_ref=dst, send_sem=snd, recv_sem=rcv,
            device_id=(pair, chol), device_id_type=MESH,
        )

    def local(ref, sem):
        return pltpu.make_async_copy(ref, ref, sem)

    def mate(k):
        z = lax.rem(z_lo + 1 - k // PLANE, 2)
        x = lax.rem(x_at + far_first(lax.rem(k // 4, 4)), 4)
        y = lax.rem(y_at + far_first(lax.rem(k, 4)), 4)
        return z * PLANE + x * 4 + y

    def line_mate(k):
        z = lax.rem(line + k, LINE)
        return lax.rem(p, PAIR // 2) + (PAIR // 2) * lax.rem(z, 2), z // 2

    far_line = (4, 3, 5, 2, 6, 1, 7)
    owner = slot == 0

    inputs = [
        pltpu.make_async_copy(src, dst, in_sem.at[i])
        for i, (src, dst) in enumerate(
            ((amps, amps_in), (fock, f_in), (eocc, e_in), (evir, ev_in), (oo, oo_in), (ov, raw))
        )
    ]
    for cp in inputs:
        cp.start()

    barrier = pltpu.get_barrier_semaphore()

    def greet(pair, chol):
        pl.semaphore_signal(barrier, inc=1, device_id=(pair, chol), device_id_type=MESH)

    for k in far_line:
        @pl.when(lax.rem(line + k, LINE) // 2 != c)
        def _(k=k):
            greet(*line_mate(k))

    @pl.loop(0, SLOTS - 1)
    def _(k):
        greet(2 * mate(k) + core, c)

    greet(peer, c)

    for cp in inputs[:3]:
        cp.wait()
    e_own = e_in[0]
    rows = [amps_in[r, :, LANES * b:LANES * (b + 1)] for r in range(2) for b in range(VB)]
    rows += [jnp.full((MSG - 2 * VB, LANES), e_own, F32)]
    msg[slot] = jnp.concatenate(rows, axis=0)
    flat = msg.reshape(PAIR * MSG, LANES)

    inputs[3].wait()
    e_vir = ev_in[...].reshape(1, V)
    f_row = f_in[...]
    poly = basis(VIR_NODES, jnp.broadcast_to(e_vir, (RANK, V)))
    gap = jnp.broadcast_to(e_vir - e_own, (RANK, V))
    turn = HALF * (gap - PAIR_MID)
    pair_poly = basis(PAIR_NODES, gap) * f_row
    f_pair = jnp.concatenate([pair_poly * jnp.cos(turn), -pair_poly * jnp.sin(turn)], axis=0)
    f_all = split(jnp.concatenate([poly * f_row, f_pair], axis=0))
    f_pair = split(f_pair)

    inputs[4].wait()
    for q in range(QUARTERS):
        oo_q[O * q:O * (q + 1), :] = oo_in[:, LANES * q:LANES * (q + 1)]
    for q in range(QUARTERS):
        at = O * q
        oo_p[at:at + 32, :] = oo_q[pl.ds(at + core, 32, stride=2), :]
        oo_p[at + 32:at + 64, :] = oo_q[pl.ds(at + 1 - core, 32, stride=2), :]
        hi, lo = split(oo_p[at:at + O, :])
        oo_hi[:, LANES * q:LANES * (q + 1)] = hi
        oo_lo[:, LANES * q:LANES * (q + 1)] = lo

    inputs[5].wait()
    for b in range(VB):
        hi, lo = split(raw[pl.ds(b, NQ, stride=VB), :])
        l_hi[:, LANES * b:LANES * (b + 1)] = hi
        l_lo[:, LANES * b:LANES * (b + 1)] = lo
    x_left[...] = dot3(f_pair, (l_hi[...], l_lo[...]), NT)

    pl.semaphore_wait(
        barrier,
        1 + (SLOTS - 1) + (LINE - 2),
    )

    f_copy = copy(f_in, f_rows.at[slot], f_snd, f_rcv, core, c)
    l_copy = copy(raw, l_other, l_snd, l_rcv, peer, c)

    @pl.when(jnp.logical_not(owner))
    def _():
        f_copy.start()

    @pl.when(owner)
    def _():
        l_copy.start()
        f_rows[0] = f_in[...]

    @pl.loop(0, SLOTS - 1)
    def _(k):
        mine = msg.at[slot, pl.ds(0, SENT)]
        copy(mine, mine, t_snd, t_rcv, 2 * mate(k) + core, c).start()

    def chunk(ref, s):
        return ref.at[pl.ds(pl.multiple_of(O * lax.rem(s, 4) + 8 * (s // 4), 8), 8)]

    def pass_on():
        @pl.loop(0, SLOTS - 1)
        def _(k):
            mine = chunk(oo_own_w, slot)
            copy(mine, mine, oa_snd, oa_rcv, 2 * mate(k) + core, c).start()

    oo_own_w = oo_g.at[0]

    @pl.when(owner)
    def _():
        @pl.loop(0, SLOTS - 1)
        def _(k):
            to = mate(k)
            copy(chunk(oo_p, to), chunk(oo_own_w, to), oc_snd, oc_rcv, 2 * to + core, c).start()

        oo_g[0, 0:8, :] = oo_p[0:8, :]
        pass_on()

    half = MSG * SLOTS
    chunks_in = oo_p.at[pl.ds(0, 8 * (SLOTS - 1))]
    local(msg.at[pl.ds(0, SLOTS - 1), pl.ds(0, SENT)], t_rcv).wait()
    t_swap = copy(msg.at[pl.ds(0, SLOTS), pl.ds(0, SENT)], msg.at[pl.ds(SLOTS, SLOTS), pl.ds(0, SENT)],
                  tp_snd, tp_rcv, peer, c)
    t_swap.start()

    def take_amps(h):
        for r in range(2):
            for b in range(VB):
                hi, lo = split(flat[pl.ds(half * h + VB * r + b, SLOTS, stride=MSG), :])
                at = slice(O * r + SLOTS * h, O * r + SLOTS * (h + 1))
                rhs_hi[at, LANES * b:LANES * (b + 1)] = hi
                rhs_lo[at, LANES * b:LANES * (b + 1)] = lo

    @pl.when(jnp.logical_not(owner))
    def _():
        local(chunk(oo_own_w, slot), oc_rcv).wait()
        pass_on()

    def project(w, slab):
        z = dot3((fm_hi[...], fm_lo[...]), slab, NT)
        for s in range(SLOTS):
            z_out[w, s] = z[RANK * s:RANK * (s + 1)]

        @pl.loop(0, SLOTS - 1)
        def _(k):
            to = mate(k)
            copy(z_out.at[w, to], z_in.at[w], z_snd.at[w], z_rcv.at[w], 2 * to + core, c).start()

        z_in[w] = z_out[w, 0]

    @pl.when(owner)
    def _():
        local(f_rows.at[pl.ds(1, SLOTS - 1)], f_rcv).wait()
        for s in range(0, SLOTS, 2):
            at = slice(RANK * s, RANK * (s + 2))
            hi, lo = split(jnp.concatenate([poly * f_rows[s], poly * f_rows[s + 1]], axis=0))
            fm_hi[at, :] = hi
            fm_lo[at, :] = lo
        project(0, (l_hi[...], l_lo[...]))
        l_copy.wait_recv()
        for b in range(VB):
            hi, lo = split(l_other[pl.ds(b, NQ, stride=VB), :])
            lx_hi[:, LANES * b:LANES * (b + 1)] = hi
            lx_lo[:, LANES * b:LANES * (b + 1)] = lo
        project(1, (lx_hi[...], lx_lo[...]))

    take_amps(0)
    t_swap.wait_recv()
    take_amps(1)

    amps_re = (rhs_hi[0:O, :], rhs_lo[0:O, :])
    amps_im = (rhs_hi[O:2 * O, :], rhs_lo[O:2 * O, :])
    tf = dot3(f_all, (rhs_hi[...], rhs_lo[...]), NT)
    tx = jnp.concatenate([tf[8:16, 0:O] - tf[16:24, O:], tf[8:16, O:] + tf[16:24, 0:O]], axis=0)
    oo_own = (oo_hi[...], oo_lo[...])
    x_terms = x_left[...] - dot3(split(tx), oo_own, NN)
    x_out[0] = x_terms[0:RANK]
    x_out[1] = x_terms[RANK:]
    x_swap = copy(x_out.at[1 - core], x_in, xp_snd, xp_rcv, peer, c)
    x_swap.start()

    e_win = [flat[half * h + EPS_AT:half * h + EPS_AT + 1, 0:1] for h in range(WIN)]
    vir_rows = e_vir + by_row(VIR_NODES, V)
    w_vir = [weight(vir_rows - (e_win[h] + e_own)) for h in range(WIN)]

    x_swap.wait_recv()
    x_sum[...] = x_out[core] + x_in[...]
    x_copy = copy(x_sum, x_all.at[slot], x_snd, x_rcv, core, c)

    @pl.when(jnp.logical_not(owner))
    def _():
        x_copy.start()

    local(chunks_in, oa_rcv).wait()
    oo_swap = copy(oo_g.at[0], oo_g.at[1], op_snd, op_rcv, peer, c)
    oo_swap.start()

    def occ_of(h):
        return jnp.concatenate([oo_g[h, O * q:O * (q + 1), :] for q in range(QUARTERS)], axis=1)

    tz = jnp.concatenate([tf[0:8, 0:O], tf[0:8, O:]], axis=0)
    tz_turned = jnp.concatenate([tz[:, O // 2:], tz[:, :O // 2]], axis=1)
    dress = [dot3(split(tz), split(occ_of(0)), NN)]
    oo_swap.wait_recv()
    dress.append(dot3(split(tz_turned), split(occ_of(1)), NN))

    def through(ct, slab, occ):
        ct = split(ct)
        lv = dot3(ct, slab, NN)
        r = split(dot3(ct, occ, NT))
        rt_re, rt_im = dot3(r, amps_re, NN), dot3(r, amps_im, NN)
        parts = []
        for g in range(0, lv.shape[0], 16):
            re, im = slice(g, g + 8), slice(g + 8, g + 16)
            parts.append((
                lv[re] - (rt_re[re] - rt_im[im]),
                lv[im] - (rt_im[re] + rt_re[im]),
            ))
        return parts

    @pl.when(jnp.logical_not(owner))
    def _():
        for w in range(WIN):
            local(z_in.at[w], z_rcv.at[w]).wait()

    cols = jnp.concatenate(
        [part for h in range(WIN) for part in (z_in[h] - dress[h][0:8], -dress[h][8:16])], axis=0)
    for h, v in enumerate(through(cols, (l_hi[...], l_lo[...]), oo_own)):
        re, im = fold(w_vir[h], v)
        om[h, :, 0:V] = -re
        om[h, :, V:2 * V] = -im
    first = copy(om.at[1], om_in, r1_snd, r1_rcv, peer, c)
    first.start()

    @pl.when(owner)
    def _():
        local(x_all.at[pl.ds(1, SLOTS - 1)], x_rcv).wait()
        total = x_sum[...]
        for k in range(1, SLOTS):
            total = total + x_all[k]
        x_tot[core] = total
        swap = copy(x_tot.at[core], x_tot.at[core], xs_snd, xs_rcv, peer, c)
        swap.start()
        w_re, w_im = weight(e_vir + by_row(PAIR_NODES, V) - e_win[0])
        turns = [HALF * (g - PAIR_MID) for g in PAIR_NODES]
        t_cos = by_row([math.cos(g) for g in turns], V)
        t_sin = by_row([math.sin(g) for g in turns], V)
        local(x_tot.at[1 - core], xs_rcv).wait()
        v, = through(jnp.concatenate([x_tot[0], x_tot[1]], axis=0), (l_hi[...], l_lo[...]), oo_own)
        re, im = fold((w_re * t_cos - w_im * t_sin, w_re * t_sin + w_im * t_cos), v)
        om[0, :, 0:V] += 2.0 * re
        om[0, :, V:2 * V] += 2.0 * im
        swap.wait_send()

    first.wait_recv()
    om_pl[plane] = om[0] + om_in[...]

    @pl.loop(PLANE, SLOTS - 1)
    def _(k):
        copy(om_pl.at[plane], om_pl.at[plane], r2_snd, r2_rcv, 2 * mate(k) + core, c).start()

    local(om_pl.at[pl.ds(0, PLANE - 1)], r2_rcv).wait()
    total = om_pl[0]
    for k in range(1, PLANE):
        total = total + om_pl[k]
    om_ln[line] = total
    for k in far_line:
        pair, chol = line_mate(k)
        copy(om_ln.at[line], om_ln.at[line], r3_snd, r3_rcv, pair, chol).start()
    local(om_ln.at[pl.ds(0, LINE - 1)], r3_rcv).wait()
    total = om_ln[0]
    for k in range(1, LINE):
        total = total + om_ln[k]
    om_fin[core] = total
    last = copy(om_fin.at[core], om_fin.at[core], r4_snd, r4_rcv, peer, c)
    last.start()
    last_in = om_fin.at[1 - core]
    local(last_in, r4_rcv).wait()
    for i in range(WIN):
        for r in range(2):
            out[r, i:i + 1, :] = om_fin[i, :, r * V:(r + 1) * V]

    last.wait_send()
    local(om_ln.at[pl.ds(0, LINE - 1)], r3_snd).wait()
    local(om_pl.at[pl.ds(0, PLANE - 1)], r2_snd).wait()
    first.wait_send()
    x_swap.wait_send()
    t_swap.wait_send()
    oo_swap.wait_send()
    local(msg.at[pl.ds(0, SLOTS - 1), pl.ds(0, SENT)], t_snd).wait()
    local(chunks_in, oa_snd).wait()

    @pl.when(jnp.logical_not(owner))
    def _():
        f_copy.wait_send()
        x_copy.wait_send()

    @pl.when(owner)
    def _():
        l_copy.wait_send()
        local(chunks_in, oc_snd).wait()
        for w in range(WIN):
            local(z_out.at[w, pl.ds(0, SLOTS - 1)], z_snd.at[w]).wait()


def per_device(chol_ov, chol_oo, amplitudes, eps_occ, eps_vir, fock):
    dma = pltpu.SemaphoreType.DMA

    def f32(*shape):
        return pltpu.VMEM(shape, F32)

    def b16(*shape):
        return pltpu.VMEM(shape, BF16)

    scratch = [
        f32(NQ * VB, LANES), f32(O, NQ), f32(2, 1, V), pltpu.SMEM((1,), F32), f32(V), f32(1, V), dma((6,)),
        f32(O * QUARTERS, LANES), f32(O * QUARTERS, LANES), b16(O, NQ), b16(O, NQ),
        b16(NQ, V), b16(NQ, V), f32(2 * RANK, NQ), f32(PAIR, MSG, LANES),
        f32(SLOTS, 1, V), f32(NQ * VB, LANES), b16(NQ, V), b16(NQ, V), f32(WIN, O * QUARTERS, LANES),
        b16(RANK * SLOTS, V), b16(RANK * SLOTS, V), b16(2 * O, V), b16(2 * O, V),
        f32(WIN, SLOTS, RANK, NQ), f32(WIN, RANK, NQ),
        f32(2, RANK, NQ), f32(RANK, NQ), f32(RANK, NQ), f32(SLOTS, RANK, NQ), f32(2, RANK, NQ),
        f32(WIN, 1, 2 * V), f32(1, 2 * V), f32(PLANE, 1, 2 * V), f32(LINE, 1, 2 * V), f32(WIN, 1, 2 * V),
        dma((WIN,)), dma((WIN,)),
    ] + [dma] * 28
    hbm = pl.BlockSpec(memory_space=pltpu.HBM)
    return pl.pallas_call(
        kernel,
        out_shape=jax.ShapeDtypeStruct((2, WIN, V), F32),
        in_specs=[hbm] * 6,
        out_specs=pl.BlockSpec(memory_space=pltpu.VMEM),
        scratch_shapes=scratch,
        compiler_params=pltpu.CompilerParams(
            collective_id=0, has_side_effects=True, vmem_limit_bytes=63 * 2**20
        ),
    )(
        chol_ov.reshape(NQ * VB, LANES), chol_oo.reshape(NQ, O).T, amplitudes, eps_occ, eps_vir, fock
    )


def solution(mesh):
    return jax.shard_map(
        per_device,
        mesh=mesh,
        in_specs=(
            P("chol", "pair", None),
            P("chol", "pair", None),
            P(None, "pair", None),
            P("pair"),
            P(),
            P("pair", None),
        ),
        out_specs=P(),
        check_vma=False,
    )
```

```python
import math

import jax
import jax.numpy as jnp
from jax import lax
from jax.experimental import pallas as pl
from jax.experimental.pallas import tpu as pltpu
from jax.sharding import PartitionSpec as P

WIN = 2
STEP_TIME = 0.7
HALF = STEP_TIME / 2
RANK = 8
VIR_LOW, VIR_HIGH = 0.3, 3.0
OCC_LOW, OCC_HIGH = -2.5, -0.4
PAIR, CHOL = 64, 4
SLOTS = PAIR // 2
PLANE = 16
LINE = 8
V, NQ, O = 768, 512, 64
LANES = 128
VB = V // LANES
QUARTERS = NQ // LANES
UNIT = LANES * VB
EPS_AT, SENT, MSG = 2 * VB, 2 * VB + 1, 16
MESH = pl.DeviceIdType.MESH
F32 = jnp.float32
BF16 = jnp.bfloat16
NN = (((1,), (0,)), ((), ()))
NT = (((1,), (1,)), ((), ()))


def nodes_on(low, high):
    mid, half = (low + high) / 2, (high - low) / 2
    return [mid + half * math.cos((2 * m + 1) * math.pi / (2 * RANK)) for m in range(RANK)]


VIR_NODES = nodes_on(VIR_LOW, VIR_HIGH)
PAIR_NODES = nodes_on(VIR_LOW - OCC_HIGH, VIR_HIGH - OCC_LOW)
PAIR_MID = (VIR_LOW - OCC_HIGH + VIR_HIGH - OCC_LOW) / 2


def by_row(values, width):
    row = lax.broadcasted_iota(jnp.int32, (RANK, width), 0)
    out = jnp.full((RANK, width), values[0], F32)
    for m in range(1, RANK):
        out = jnp.where(row == m, F32(values[m]), out)
    return out


def basis(nodes, at):
    scale = []
    for m in range(RANK):
        den = 1.0
        for n in range(RANK):
            if n != m:
                den *= nodes[m] - nodes[n]
        scale.append(1.0 / den)
    width = at.shape[1]
    row = lax.broadcasted_iota(jnp.int32, (RANK, width), 0)
    out = by_row(scale, width)
    for n in range(RANK):
        out = out * jnp.where(row == n, F32(1.0), at - F32(nodes[n]))
    return out


def weight(denom):
    s, c = jnp.sin(HALF * denom), jnp.cos(HALF * denom)
    q = 2.0 * s / denom
    return q * s, q * c


def fold(w, v):
    re = jnp.sum(w[0] * v[0] - w[1] * v[1], axis=0, keepdims=True)
    im = jnp.sum(w[0] * v[1] + w[1] * v[0], axis=0, keepdims=True)
    return re, im


def split(x):
    hi = x.astype(BF16)
    return hi, (x - hi.astype(F32)).astype(BF16)


def dot(a, b, dims):
    return lax.dot_general(a, b, dims, preferred_element_type=F32)


def dot3(a, b, dims):
    a_hi, a_lo = a
    b_hi, b_lo = b
    rows = a_hi.shape[0]
    both = dot(jnp.concatenate([a_hi, a_lo], axis=0), b_hi, dims)
    return both[:rows] + both[rows:] + dot(a_hi, b_lo, dims)


RING = (0, 1, 2, 1)
DIRECT = sorted(
    (at for at in range(1, SLOTS) if at < PLANE or at % 2 == 0),
    key=lambda at: -(at // PLANE + RING[at // 4 % 4] + RING[at % 4]),
)


def held_at(at):
    return at if at < PLANE else PLANE + 4 * (at % 4) + (at - PLANE) // 4


def far_first(v):
    return 2 + v - (v // 2) * (2 * v - 1)


def kernel(
    ov, oo, amps, eocc, evir, fock, out,
    raw, oo_in, amps_in, e_in, ev_in, f_in, in_sem,
    oo_q, oo_p, oo_hi, oo_lo, l_hi, l_lo, x_left, msg,
    f_rows, l_other, lx_hi, lx_lo, oo_g, fm_hi, fm_lo, rhs_hi, rhs_lo, z_out, z_in, z_held,
    x_out, x_in, x_sum, x_row, x_head, x_all, x_tot, om, om_in, om_pl, om_ln, om_fin,
    z_snd, z_rcv, zh_rcv, zh_snd, xr_rcv, xh_snd, l_snd, l_rcv, f_snd, f_rcv, x_snd, x_rcv, xs_snd, xs_rcv, t_snd, t_rcv, tp_snd, tp_rcv,
    oc_snd, oc_rcv, oa_snd, oa_rcv, op_snd, op_rcv, xp_snd, xp_rcv, r1_snd, r1_rcv, r2_snd, r2_rcv, r3_snd, r3_rcv, r4_snd, r4_rcv,
):
    p, c = lax.axis_index("pair"), lax.axis_index("chol")
    core = lax.rem(p, 2)
    slot = p // 2
    peer = p + 1 - 2 * core
    z_lo, x_at, y_at = slot // PLANE, lax.rem(slot // 4, 4), lax.rem(slot, 4)
    plane = lax.rem(slot, PLANE)
    line = 2 * c + z_lo

    def copy(src, dst, snd, rcv, pair, chol):
        return pltpu.make_async_remote_copy(
            src_ref=src, dst_ref=dst, send_sem=snd, recv_sem=rcv,
            device_id=(pair, chol), device_id_type=MESH,
        )

    def local(ref, sem):
        return pltpu.make_async_copy(ref, ref, sem)

    def mate(k):
        z = lax.rem(z_lo + 1 - k // PLANE, 2)
        x = lax.rem(x_at + far_first(lax.rem(k // 4, 4)), 4)
        y = lax.rem(y_at + far_first(lax.rem(k, 4)), 4)
        return z * PLANE + x * 4 + y

    def line_mate(k):
        z = lax.rem(line + k, LINE)
        return lax.rem(p, PAIR // 2) + (PAIR // 2) * lax.rem(z, 2), z // 2

    far_line = (4, 3, 5, 2, 6, 1, 7)
    owner = slot == 0
    head = slot < 4
    relay = (slot == 1) | (slot == 3)

    inputs = [
        pltpu.make_async_copy(src, dst, in_sem.at[i])
        for i, (src, dst) in enumerate(
            ((amps, amps_in), (fock, f_in), (eocc, e_in), (evir, ev_in), (oo, oo_in), (ov, raw))
        )
    ]
    for cp in inputs:
        cp.start()

    barrier = pltpu.get_barrier_semaphore()

    def greet(pair, chol):
        pl.semaphore_signal(barrier, inc=1, device_id=(pair, chol), device_id_type=MESH)

    for k in far_line:
        @pl.when(lax.rem(line + k, LINE) // 2 != c)
        def _(k=k):
            greet(*line_mate(k))

    @pl.loop(0, SLOTS - 1)
    def _(k):
        greet(2 * mate(k) + core, c)

    greet(peer, c)

    for cp in inputs[:3]:
        cp.wait()
    e_own = e_in[0]
    rows = [amps_in[r, :, LANES * b:LANES * (b + 1)] for r in range(2) for b in range(VB)]
    rows += [jnp.full((MSG - 2 * VB, LANES), e_own, F32)]
    msg[slot] = jnp.concatenate(rows, axis=0)
    flat = msg.reshape(PAIR * MSG, LANES)

    inputs[3].wait()
    e_vir = ev_in[...].reshape(1, V)
    f_row = f_in[...]
    poly = basis(VIR_NODES, jnp.broadcast_to(e_vir, (RANK, V)))
    gap = jnp.broadcast_to(e_vir - e_own, (RANK, V))
    turn = HALF * (gap - PAIR_MID)
    pair_poly = basis(PAIR_NODES, gap) * f_row
    f_pair = jnp.concatenate([pair_poly * jnp.cos(turn), -pair_poly * jnp.sin(turn)], axis=0)
    f_all = split(jnp.concatenate([poly * f_row, f_pair], axis=0))
    f_pair = split(f_pair)

    inputs[4].wait()
    for q in range(QUARTERS):
        oo_q[O * q:O * (q + 1), :] = oo_in[:, LANES * q:LANES * (q + 1)]
    for q in range(QUARTERS):
        at = O * q
        oo_p[at:at + 32, :] = oo_q[pl.ds(at + core, 32, stride=2), :]
        oo_p[at + 32:at + 64, :] = oo_q[pl.ds(at + 1 - core, 32, stride=2), :]
        hi, lo = split(oo_p[at:at + O, :])
        oo_hi[:, LANES * q:LANES * (q + 1)] = hi
        oo_lo[:, LANES * q:LANES * (q + 1)] = lo

    inputs[5].wait()
    for b in range(VB):
        hi, lo = split(raw[pl.ds(b, NQ, stride=VB), :])
        l_hi[:, LANES * b:LANES * (b + 1)] = hi
        l_lo[:, LANES * b:LANES * (b + 1)] = lo
    x_left[...] = dot3(f_pair, (l_hi[...], l_lo[...]), NT)

    pl.semaphore_wait(
        barrier,
        1 + (SLOTS - 1) + (LINE - 2),
    )

    f_copy = copy(f_in, f_rows.at[slot], f_snd, f_rcv, core, c)
    l_copy = copy(raw, l_other, l_snd, l_rcv, peer, c)

    @pl.when(jnp.logical_not(owner))
    def _():
        f_copy.start()

    @pl.when(owner)
    def _():
        l_copy.start()
        f_rows[0] = f_in[...]

    @pl.loop(0, SLOTS - 1)
    def _(k):
        mine = msg.at[slot, pl.ds(0, SENT)]
        copy(mine, mine, t_snd, t_rcv, 2 * mate(k) + core, c).start()

    def chunk(ref, s):
        return ref.at[pl.ds(pl.multiple_of(O * lax.rem(s, 4) + 8 * (s // 4), 8), 8)]

    def pass_on():
        @pl.loop(0, SLOTS - 1)
        def _(k):
            mine = chunk(oo_own_w, slot)
            copy(mine, mine, oa_snd, oa_rcv, 2 * mate(k) + core, c).start()

    oo_own_w = oo_g.at[0]

    @pl.when(owner)
    def _():
        @pl.loop(0, SLOTS - 1)
        def _(k):
            to = mate(k)
            copy(chunk(oo_p, to), chunk(oo_own_w, to), oc_snd, oc_rcv, 2 * to + core, c).start()

        oo_g[0, 0:8, :] = oo_p[0:8, :]
        pass_on()

    half = MSG * SLOTS
    chunks_in = oo_p.at[pl.ds(0, 8 * (SLOTS - 1))]
    local(msg.at[pl.ds(0, SLOTS - 1), pl.ds(0, SENT)], t_rcv).wait()
    t_swap = copy(msg.at[pl.ds(0, SLOTS), pl.ds(0, SENT)], msg.at[pl.ds(SLOTS, SLOTS), pl.ds(0, SENT)],
                  tp_snd, tp_rcv, peer, c)
    t_swap.start()

    def take_amps(h):
        for r in range(2):
            for b in range(VB):
                hi, lo = split(flat[pl.ds(half * h + VB * r + b, SLOTS, stride=MSG), :])
                at = slice(O * r + SLOTS * h, O * r + SLOTS * (h + 1))
                rhs_hi[at, LANES * b:LANES * (b + 1)] = hi
                rhs_lo[at, LANES * b:LANES * (b + 1)] = lo

    @pl.when(jnp.logical_not(owner))
    def _():
        local(chunk(oo_own_w, slot), oc_rcv).wait()
        pass_on()

    def project(w, slab):
        z = dot3((fm_hi[...], fm_lo[...]), slab, NT)
        for s in range(SLOTS):
            z_out[w, held_at(s)] = z[RANK * s:RANK * (s + 1)]
        for y in (1, 3):
            block = z_out.at[w, pl.ds(PLANE + 4 * y, 4)]
            copy(block, z_held.at[w], z_snd.at[w], zh_rcv.at[w], 2 * y + core, c).start()
        for to in DIRECT:
            copy(z_out.at[w, held_at(to)], z_in.at[w], z_snd.at[w], z_rcv.at[w], 2 * to + core, c).start()
        z_in[w] = z_out[w, 0]

    @pl.when(owner)
    def _():
        local(f_rows.at[pl.ds(1, SLOTS - 1)], f_rcv).wait()
        for s in range(0, SLOTS, 2):
            at = slice(RANK * s, RANK * (s + 2))
            hi, lo = split(jnp.concatenate([poly * f_rows[s], poly * f_rows[s + 1]], axis=0))
            fm_hi[at, :] = hi
            fm_lo[at, :] = lo
        project(0, (l_hi[...], l_lo[...]))
        l_copy.wait_recv()
        for b in range(VB):
            hi, lo = split(l_other[pl.ds(b, NQ, stride=VB), :])
            lx_hi[:, LANES * b:LANES * (b + 1)] = hi
            lx_lo[:, LANES * b:LANES * (b + 1)] = lo
        project(1, (lx_hi[...], lx_lo[...]))

    take_amps(0)
    t_swap.wait_recv()
    take_amps(1)

    amps_re = (rhs_hi[0:O, :], rhs_lo[0:O, :])
    amps_im = (rhs_hi[O:2 * O, :], rhs_lo[O:2 * O, :])
    tf = dot3(f_all, (rhs_hi[...], rhs_lo[...]), NT)
    tx = jnp.concatenate([tf[8:16, 0:O] - tf[16:24, O:], tf[8:16, O:] + tf[16:24, 0:O]], axis=0)
    oo_own = (oo_hi[...], oo_lo[...])
    x_terms = x_left[...] - dot3(split(tx), oo_own, NN)
    x_out[0] = x_terms[0:RANK]
    x_out[1] = x_terms[RANK:]
    x_swap = copy(x_out.at[1 - core], x_in, xp_snd, xp_rcv, peer, c)
    x_swap.start()

    e_win = [flat[half * h + EPS_AT:half * h + EPS_AT + 1, 0:1] for h in range(WIN)]
    vir_rows = e_vir + by_row(VIR_NODES, V)
    w_vir = [weight(vir_rows - (e_win[h] + e_own)) for h in range(WIN)]

    x_swap.wait_recv()
    x_sum[...] = x_out[core] + x_in[...]
    x_copy = copy(x_sum, x_row.at[slot // 4], x_snd, xr_rcv, 2 * y_at + core, c)
    head_copy = copy(x_head, x_all.at[slot], xh_snd, x_rcv, core, c)

    @pl.when(jnp.logical_not(head))
    def _():
        x_copy.start()

    @pl.when(relay)
    def _():
        for w in range(WIN):
            local(z_held.at[w], zh_rcv.at[w]).wait()
            for x in range(4):
                copy(z_held.at[w, x], z_in.at[w], zh_snd, z_rcv.at[w], 2 * (PLANE + 4 * x) + p, c).start()

    @pl.when(head)
    def _():
        local(x_row.at[pl.ds(1, 7)], xr_rcv).wait()
        total = x_sum[...]
        for k in range(1, 8):
            total = total + x_row[k]
        x_head[...] = total

        @pl.when(jnp.logical_not(owner))
        def _():
            head_copy.start()

    local(chunks_in, oa_rcv).wait()
    oo_swap = copy(oo_g.at[0], oo_g.at[1], op_snd, op_rcv, peer, c)
    oo_swap.start()

    def occ_of(h):
        return jnp.concatenate([oo_g[h, O * q:O * (q + 1), :] for q in range(QUARTERS)], axis=1)

    tz = jnp.concatenate([tf[0:8, 0:O], tf[0:8, O:]], axis=0)
    tz_turned = jnp.concatenate([tz[:, O // 2:], tz[:, :O // 2]], axis=1)
    dress = [dot3(split(tz), split(occ_of(0)), NN)]
    oo_swap.wait_recv()
    dress.append(dot3(split(tz_turned), split(occ_of(1)), NN))

    def through(ct, slab, occ):
        ct = split(ct)
        lv = dot3(ct, slab, NN)
        r = split(dot3(ct, occ, NT))
        rt_re, rt_im = dot3(r, amps_re, NN), dot3(r, amps_im, NN)
        parts = []
        for g in range(0, lv.shape[0], 16):
            re, im = slice(g, g + 8), slice(g + 8, g + 16)
            parts.append((
                lv[re] - (rt_re[re] - rt_im[im]),
                lv[im] - (rt_im[re] + rt_re[im]),
            ))
        return parts

    @pl.when(jnp.logical_not(owner))
    def _():
        for w in range(WIN):
            local(z_in.at[w], z_rcv.at[w]).wait()

    cols = jnp.concatenate(
        [part for h in range(WIN) for part in (z_in[h] - dress[h][0:8], -dress[h][8:16])], axis=0)
    for h, v in enumerate(through(cols, (l_hi[...], l_lo[...]), oo_own)):
        re, im = fold(w_vir[h], v)
        om[h, :, 0:V] = -re
        om[h, :, V:2 * V] = -im
    first = copy(om.at[1], om_in, r1_snd, r1_rcv, peer, c)
    first.start()

    @pl.when(owner)
    def _():
        local(x_all.at[pl.ds(1, 3)], x_rcv).wait()
        x_tot[core] = x_head[...] + x_all[1] + x_all[2] + x_all[3]
        swap = copy(x_tot.at[core], x_tot.at[core], xs_snd, xs_rcv, peer, c)
        swap.start()
        w_re, w_im = weight(e_vir + by_row(PAIR_NODES, V) - e_win[0])
        turns = [HALF * (g - PAIR_MID) for g in PAIR_NODES]
        t_cos = by_row([math.cos(g) for g in turns], V)
        t_sin = by_row([math.sin(g) for g in turns], V)
        local(x_tot.at[1 - core], xs_rcv).wait()
        v, = through(jnp.concatenate([x_tot[0], x_tot[1]], axis=0), (l_hi[...], l_lo[...]), oo_own)
        re, im = fold((w_re * t_cos - w_im * t_sin, w_re * t_sin + w_im * t_cos), v)
        om[0, :, 0:V] += 2.0 * re
        om[0, :, V:2 * V] += 2.0 * im
        swap.wait_send()

    first.wait_recv()
    om_pl[plane] = om[0] + om_in[...]

    @pl.loop(PLANE, SLOTS - 1)
    def _(k):
        copy(om_pl.at[plane], om_pl.at[plane], r2_snd, r2_rcv, 2 * mate(k) + core, c).start()

    local(om_pl.at[pl.ds(0, PLANE - 1)], r2_rcv).wait()
    total = om_pl[0]
    for k in range(1, PLANE):
        total = total + om_pl[k]
    om_ln[line] = total
    for k in far_line:
        pair, chol = line_mate(k)
        copy(om_ln.at[line], om_ln.at[line], r3_snd, r3_rcv, pair, chol).start()
    local(om_ln.at[pl.ds(0, LINE - 1)], r3_rcv).wait()
    total = om_ln[0]
    for k in range(1, LINE):
        total = total + om_ln[k]
    om_fin[core] = total
    last = copy(om_fin.at[core], om_fin.at[core], r4_snd, r4_rcv, peer, c)
    last.start()
    last_in = om_fin.at[1 - core]
    local(last_in, r4_rcv).wait()
    for i in range(WIN):
        for r in range(2):
            out[r, i:i + 1, :] = om_fin[i, :, r * V:(r + 1) * V]

    last.wait_send()
    local(om_ln.at[pl.ds(0, LINE - 1)], r3_snd).wait()
    local(om_pl.at[pl.ds(0, PLANE - 1)], r2_snd).wait()
    first.wait_send()
    x_swap.wait_send()
    t_swap.wait_send()
    oo_swap.wait_send()
    local(msg.at[pl.ds(0, SLOTS - 1), pl.ds(0, SENT)], t_snd).wait()
    local(chunks_in, oa_snd).wait()

    @pl.when(jnp.logical_not(owner))
    def _():
        f_copy.wait_send()

    @pl.when(jnp.logical_not(head))
    def _():
        x_copy.wait_send()

    @pl.when(head & jnp.logical_not(owner))
    def _():
        head_copy.wait_send()

    @pl.when(relay)
    def _():
        local(z_held, zh_snd).wait()

    @pl.when(owner)
    def _():
        l_copy.wait_send()
        local(chunks_in, oc_snd).wait()
        for w in range(WIN):
            local(z_out.at[w, pl.ds(0, SLOTS - 1)], z_snd.at[w]).wait()


def per_device(chol_ov, chol_oo, amplitudes, eps_occ, eps_vir, fock):
    dma = pltpu.SemaphoreType.DMA

    def f32(*shape):
        return pltpu.VMEM(shape, F32)

    def b16(*shape):
        return pltpu.VMEM(shape, BF16)

    scratch = [
        f32(NQ * VB, LANES), f32(O, NQ), f32(2, 1, V), pltpu.SMEM((1,), F32), f32(V), f32(1, V), dma((6,)),
        f32(O * QUARTERS, LANES), f32(O * QUARTERS, LANES), b16(O, NQ), b16(O, NQ),
        b16(NQ, V), b16(NQ, V), f32(2 * RANK, NQ), f32(PAIR, MSG, LANES),
        f32(SLOTS, 1, V), f32(NQ * VB, LANES), b16(NQ, V), b16(NQ, V), f32(WIN, O * QUARTERS, LANES),
        b16(RANK * SLOTS, V), b16(RANK * SLOTS, V), b16(2 * O, V), b16(2 * O, V),
        f32(WIN, SLOTS, RANK, NQ), f32(WIN, RANK, NQ), f32(WIN, 4, RANK, NQ),
        f32(2, RANK, NQ), f32(RANK, NQ), f32(RANK, NQ), f32(8, RANK, NQ), f32(RANK, NQ),
        f32(4, RANK, NQ), f32(2, RANK, NQ),
        f32(WIN, 1, 2 * V), f32(1, 2 * V), f32(PLANE, 1, 2 * V), f32(LINE, 1, 2 * V), f32(WIN, 1, 2 * V),
        dma((WIN,)), dma((WIN,)), dma((WIN,)),
    ] + [dma] * 31
    hbm = pl.BlockSpec(memory_space=pltpu.HBM)
    return pl.pallas_call(
        kernel,
        out_shape=jax.ShapeDtypeStruct((2, WIN, V), F32),
        in_specs=[hbm] * 6,
        out_specs=pl.BlockSpec(memory_space=pltpu.VMEM),
        scratch_shapes=scratch,
        compiler_params=pltpu.CompilerParams(
            collective_id=0, has_side_effects=True, vmem_limit_bytes=63 * 2**20
        ),
    )(
        chol_ov.reshape(NQ * VB, LANES), chol_oo.reshape(NQ, O).T, amplitudes, eps_occ, eps_vir, fock
    )


def solution(mesh):
    return jax.shard_map(
        per_device,
        mesh=mesh,
        in_specs=(
            P("chol", "pair", None),
            P("chol", "pair", None),
            P(None, "pair", None),
            P("pair"),
            P(),
            P("pair", None),
        ),
        out_specs=P(),
        check_vma=False,
    )
```

```python
import math

import jax
import jax.numpy as jnp
from jax import lax
from jax.experimental import pallas as pl
from jax.experimental.pallas import tpu as pltpu
from jax.sharding import PartitionSpec as P

WIN = 2
STEP_TIME = 0.7
HALF = STEP_TIME / 2
RANK = 8
VIR_LOW, VIR_HIGH = 0.3, 3.0
OCC_LOW, OCC_HIGH = -2.5, -0.4
PAIR, CHOL = 64, 4
SLOTS = PAIR // 2
PLANE = 16
LINE = 8
V, NQ, O = 768, 512, 64
LANES = 128
VB = V // LANES
QUARTERS = NQ // LANES
UNIT = LANES * VB
EPS_AT, SENT, MSG = 2 * VB, 2 * VB + 1, 16
MESH = pl.DeviceIdType.MESH
F32 = jnp.float32
BF16 = jnp.bfloat16
NN = (((1,), (0,)), ((), ()))
NT = (((1,), (1,)), ((), ()))


def nodes_on(low, high):
    mid, half = (low + high) / 2, (high - low) / 2
    return [mid + half * math.cos((2 * m + 1) * math.pi / (2 * RANK)) for m in range(RANK)]


VIR_NODES = nodes_on(VIR_LOW, VIR_HIGH)
PAIR_NODES = nodes_on(VIR_LOW - OCC_HIGH, VIR_HIGH - OCC_LOW)
PAIR_MID = (VIR_LOW - OCC_HIGH + VIR_HIGH - OCC_LOW) / 2


def by_row(values, width):
    row = lax.broadcasted_iota(jnp.int32, (RANK, width), 0)
    out = jnp.full((RANK, width), values[0], F32)
    for m in range(1, RANK):
        out = jnp.where(row == m, F32(values[m]), out)
    return out


def basis(nodes, at):
    scale = []
    for m in range(RANK):
        den = 1.0
        for n in range(RANK):
            if n != m:
                den *= nodes[m] - nodes[n]
        scale.append(1.0 / den)
    width = at.shape[1]
    row = lax.broadcasted_iota(jnp.int32, (RANK, width), 0)
    out = by_row(scale, width)
    for n in range(RANK):
        out = out * jnp.where(row == n, F32(1.0), at - F32(nodes[n]))
    return out


def weight(denom):
    s, c = jnp.sin(HALF * denom), jnp.cos(HALF * denom)
    q = 2.0 * s / denom
    return q * s, q * c


def fold(w, v):
    re = jnp.sum(w[0] * v[0] - w[1] * v[1], axis=0, keepdims=True)
    im = jnp.sum(w[0] * v[1] + w[1] * v[0], axis=0, keepdims=True)
    return re, im


def split(x):
    hi = x.astype(BF16)
    return hi, (x - hi.astype(F32)).astype(BF16)


def dot(a, b, dims):
    return lax.dot_general(a, b, dims, preferred_element_type=F32)


def dot3(a, b, dims):
    a_hi, a_lo = a
    b_hi, b_lo = b
    rows = a_hi.shape[0]
    both = dot(jnp.concatenate([a_hi, a_lo], axis=0), b_hi, dims)
    return both[:rows] + both[rows:] + dot(a_hi, b_lo, dims)


RING = (0, 1, 2, 1)
DIRECT = sorted(
    (at for at in range(1, SLOTS) if at < PLANE or at % 2 == 0),
    key=lambda at: -(at // PLANE + RING[at // 4 % 4] + RING[at % 4]),
)


def held_at(at):
    return at if at < PLANE else PLANE + 4 * (at % 4) + (at - PLANE) // 4


def far_first(v):
    return 2 + v - (v // 2) * (2 * v - 1)


def kernel(
    ov, oo, amps, eocc, evir, fock, out,
    raw, oo_in, amps_in, e_in, ev_in, f_in, in_sem,
    oo_q, oo_p, oo_hi, oo_lo, l_hi, l_lo, x_left, msg,
    parcel_out, parcel, f_rows, l_other, lx_hi, lx_lo, oo_g, fm_hi, fm_lo, rhs_hi, rhs_lo, z_out, z_in, z_held,
    x_out, x_in, x_sum, x_row, x_head, x_all, x_tot, om, om_in, om_pl, om_ln, om_fin,
    z_snd, z_rcv, zh_rcv, zh_snd, xr_rcv, xh_snd, l_snd, l_rcv, f_snd, f_rcv, x_snd, x_rcv, xs_snd, xs_rcv, t_snd, t_rcv, tp_snd, tp_rcv,
    oc_snd, oc_rcv, oa_snd, oa_rcv, op_snd, op_rcv, xp_snd, xp_rcv, r1_snd, r1_rcv, r2_snd, r2_rcv, r3_snd, r3_rcv, r4_snd, r4_rcv,
):
    p, c = lax.axis_index("pair"), lax.axis_index("chol")
    core = lax.rem(p, 2)
    slot = p // 2
    peer = p + 1 - 2 * core
    z_lo, x_at, y_at = slot // PLANE, lax.rem(slot // 4, 4), lax.rem(slot, 4)
    plane = lax.rem(slot, PLANE)
    line = 2 * c + z_lo

    def copy(src, dst, snd, rcv, pair, chol):
        return pltpu.make_async_remote_copy(
            src_ref=src, dst_ref=dst, send_sem=snd, recv_sem=rcv,
            device_id=(pair, chol), device_id_type=MESH,
        )

    def local(ref, sem):
        return pltpu.make_async_copy(ref, ref, sem)

    def mate(k):
        z = lax.rem(z_lo + 1 - k // PLANE, 2)
        x = lax.rem(x_at + far_first(lax.rem(k // 4, 4)), 4)
        y = lax.rem(y_at + far_first(lax.rem(k, 4)), 4)
        return z * PLANE + x * 4 + y

    def line_mate(k):
        z = lax.rem(line + k, LINE)
        return lax.rem(p, PAIR // 2) + (PAIR // 2) * lax.rem(z, 2), z // 2

    far_line = (4, 3, 5, 2, 6, 1, 7)
    owner = slot == 0
    head = slot < 4
    relay = (slot == 1) | (slot == 3)

    inputs = [
        pltpu.make_async_copy(src, dst, in_sem.at[i])
        for i, (src, dst) in enumerate(
            ((amps, amps_in), (fock, f_in), (eocc, e_in), (evir, ev_in), (oo, oo_in), (ov, raw))
        )
    ]
    for cp in inputs:
        cp.start()

    barrier = pltpu.get_barrier_semaphore()

    def greet(pair, chol):
        pl.semaphore_signal(barrier, inc=1, device_id=(pair, chol), device_id_type=MESH)

    @pl.loop(0, SLOTS - 1)
    def _(k):
        greet(2 * mate(k) + core, c)

    greet(peer, c)

    for k in far_line:
        @pl.when(lax.rem(line + k, LINE) // 2 != c)
        def _(k=k):
            greet(*line_mate(k))

    for cp in inputs[:3]:
        cp.wait()
    e_own = e_in[0]
    rows = [amps_in[r, :, LANES * b:LANES * (b + 1)] for r in range(2) for b in range(VB)]
    rows += [jnp.full((MSG - 2 * VB, LANES), e_own, F32)]
    msg[slot] = jnp.concatenate(rows, axis=0)
    flat = msg.reshape(PAIR * MSG, LANES)

    inputs[3].wait()
    e_vir = ev_in[...].reshape(1, V)
    f_row = f_in[...]
    poly = basis(VIR_NODES, jnp.broadcast_to(e_vir, (RANK, V)))
    gap = jnp.broadcast_to(e_vir - e_own, (RANK, V))
    turn = HALF * (gap - PAIR_MID)
    pair_poly = basis(PAIR_NODES, gap) * f_row
    f_pair = jnp.concatenate([pair_poly * jnp.cos(turn), -pair_poly * jnp.sin(turn)], axis=0)
    f_all = split(jnp.concatenate([poly * f_row, f_pair], axis=0))
    f_pair = split(f_pair)

    inputs[4].wait()
    for q in range(QUARTERS):
        oo_q[O * q:O * (q + 1), :] = oo_in[:, LANES * q:LANES * (q + 1)]
    for q in range(QUARTERS):
        at = O * q
        oo_p[at:at + 32, :] = oo_q[pl.ds(at + core, 32, stride=2), :]
        oo_p[at + 32:at + 64, :] = oo_q[pl.ds(at + 1 - core, 32, stride=2), :]
        hi, lo = split(oo_p[at:at + O, :])
        oo_hi[:, LANES * q:LANES * (q + 1)] = hi
        oo_lo[:, LANES * q:LANES * (q + 1)] = lo

    @pl.when(owner)
    def _():
        for to in range(1, SLOTS):
            at = O * (to % 4) + 8 * (to // 4)
            parcel_out[to, 0:8] = oo_p[at:at + 8, :]
            parcel_out[to, 8:8 + MSG] = msg[0]

    inputs[5].wait()
    for b in range(VB):
        hi, lo = split(raw[pl.ds(b, NQ, stride=VB), :])
        l_hi[:, LANES * b:LANES * (b + 1)] = hi
        l_lo[:, LANES * b:LANES * (b + 1)] = lo
    x_left[...] = dot3(f_pair, (l_hi[...], l_lo[...]), NT)

    pl.semaphore_wait(
        barrier,
        1 + (SLOTS - 1) + (LINE - 2),
    )

    f_copy = copy(f_in, f_rows.at[slot], f_snd, f_rcv, core, c)
    l_copy = copy(raw, l_other, l_snd, l_rcv, peer, c)

    @pl.when(jnp.logical_not(owner))
    def _():
        f_copy.start()

    @pl.when(owner)
    def _():
        l_copy.start()
        f_rows[0] = f_in[...]

    @pl.when(jnp.logical_not(owner))
    def _():
        @pl.loop(0, SLOTS - 1)
        def _(k):
            mine = msg.at[slot, pl.ds(0, SENT)]
            copy(mine, mine, t_snd, t_rcv, 2 * mate(k) + core, c).start()

    def pass_on(mine, into):
        @pl.loop(0, SLOTS - 1)
        def _(k):
            copy(mine, into, oa_snd, oa_rcv, 2 * mate(k) + core, c).start()

    oo_own_w = oo_g.at[0]

    def own_chunk(at):
        return oo_own_w.at[pl.ds(at, 8)]

    @pl.when(owner)
    def _():
        for to in sorted(range(1, SLOTS), key=lambda at: -(at // PLANE + RING[at // 4 % 4] + RING[at % 4])):
            copy(parcel_out.at[to], parcel, oc_snd, oc_rcv, 2 * to + core, c).start()

        oo_g[0, 0:8, :] = oo_p[0:8, :]
        pass_on(own_chunk(0), own_chunk(0))

    half = MSG * SLOTS
    chunks_in = oo_p.at[pl.ds(0, 8 * (SLOTS - 1))]
    @pl.when(jnp.logical_not(owner))
    def _():
        local(msg.at[pl.ds(0, SLOTS - 2), pl.ds(0, SENT)], t_rcv).wait()
        local(parcel, oc_rcv).wait()
        msg[0] = parcel[8:8 + MSG]

    t_swap = copy(msg.at[pl.ds(0, SLOTS), pl.ds(0, SENT)], msg.at[pl.ds(SLOTS, SLOTS), pl.ds(0, SENT)],
                  tp_snd, tp_rcv, peer, c)

    @pl.when(jnp.logical_not(owner))
    def _():
        t_swap.start()

    def take_amps(h):
        for r in range(2):
            for b in range(VB):
                hi, lo = split(flat[pl.ds(half * h + VB * r + b, SLOTS, stride=MSG), :])
                at = slice(O * r + SLOTS * h, O * r + SLOTS * (h + 1))
                rhs_hi[at, LANES * b:LANES * (b + 1)] = hi
                rhs_lo[at, LANES * b:LANES * (b + 1)] = lo

    @pl.when(jnp.logical_not(owner))
    def _():
        at = pl.multiple_of(O * lax.rem(slot, 4) + 8 * (slot // 4), 8)
        oo_g[0, pl.ds(at, 8), :] = parcel[0:8]
        pass_on(parcel.at[pl.ds(0, 8)], own_chunk(at))

    def project(w, slab):
        z = dot3((fm_hi[...], fm_lo[...]), slab, NT)
        for s in range(SLOTS):
            z_out[w, held_at(s)] = z[RANK * s:RANK * (s + 1)]
        for y in (1, 3):
            block = z_out.at[w, pl.ds(PLANE + 4 * y, 4)]
            copy(block, z_held.at[w], z_snd.at[w], zh_rcv.at[w], 2 * y + core, c).start()
        for to in DIRECT:
            copy(z_out.at[w, held_at(to)], z_in.at[w], z_snd.at[w], z_rcv.at[w], 2 * to + core, c).start()
        z_in[w] = z_out[w, 0]

    @pl.when(owner)
    def _():
        l_copy.wait_recv()
        for b in range(VB):
            hi, lo = split(l_other[pl.ds(b, NQ, stride=VB), :])
            lx_hi[:, LANES * b:LANES * (b + 1)] = hi
            lx_lo[:, LANES * b:LANES * (b + 1)] = lo
        local(f_rows.at[pl.ds(1, SLOTS - 1)], f_rcv).wait()
        for s in range(0, SLOTS, 2):
            at = slice(RANK * s, RANK * (s + 2))
            hi, lo = split(jnp.concatenate([poly * f_rows[s], poly * f_rows[s + 1]], axis=0))
            fm_hi[at, :] = hi
            fm_lo[at, :] = lo
        project(0, (l_hi[...], l_lo[...]))
        local(msg.at[pl.ds(0, SLOTS - 1), pl.ds(0, SENT)], t_rcv).wait()
        t_swap.start()
        project(1, (lx_hi[...], lx_lo[...]))

    take_amps(0)
    t_swap.wait_recv()
    take_amps(1)

    amps_re = (rhs_hi[0:O, :], rhs_lo[0:O, :])
    amps_im = (rhs_hi[O:2 * O, :], rhs_lo[O:2 * O, :])
    tf = dot3(f_all, (rhs_hi[...], rhs_lo[...]), NT)
    tx = jnp.concatenate([tf[8:16, 0:O] - tf[16:24, O:], tf[8:16, O:] + tf[16:24, 0:O]], axis=0)
    oo_own = (oo_hi[...], oo_lo[...])
    x_terms = x_left[...] - dot3(split(tx), oo_own, NN)
    x_out[0] = x_terms[0:RANK]
    x_out[1] = x_terms[RANK:]
    x_swap = copy(x_out.at[1 - core], x_in, xp_snd, xp_rcv, peer, c)
    x_swap.start()

    e_win = [flat[half * h + EPS_AT:half * h + EPS_AT + 1, 0:1] for h in range(WIN)]
    vir_rows = e_vir + by_row(VIR_NODES, V)
    w_vir = [weight(vir_rows - (e_win[h] + e_own)) for h in range(WIN)]

    @pl.when(relay)
    def _():
        for w in (0,):
            local(z_held.at[w], zh_rcv.at[w]).wait()
            for x in range(4):
                copy(z_held.at[w, x], z_in.at[w], zh_snd, z_rcv.at[w], 2 * (PLANE + 4 * x) + p, c).start()

    x_swap.wait_recv()
    x_sum[...] = x_out[core] + x_in[...]
    x_copy = copy(x_sum, x_row.at[slot // 4], x_snd, xr_rcv, 2 * y_at + core, c)
    head_copy = copy(x_head, x_all.at[slot], xh_snd, x_rcv, core, c)

    @pl.when(jnp.logical_not(head))
    def _():
        x_copy.start()

    @pl.when(relay)
    def _():
        for w in (1,):
            local(z_held.at[w], zh_rcv.at[w]).wait()
            for x in range(4):
                copy(z_held.at[w, x], z_in.at[w], zh_snd, z_rcv.at[w], 2 * (PLANE + 4 * x) + p, c).start()

    @pl.when(head)
    def _():
        local(x_row.at[pl.ds(1, 7)], xr_rcv).wait()
        total = x_sum[...]
        for k in range(1, 8):
            total = total + x_row[k]
        x_head[...] = total

        @pl.when(jnp.logical_not(owner))
        def _():
            head_copy.start()

    local(chunks_in, oa_rcv).wait()
    oo_swap = copy(oo_g.at[0], oo_g.at[1], op_snd, op_rcv, peer, c)
    oo_swap.start()

    def occ_of(h):
        return jnp.concatenate([oo_g[h, O * q:O * (q + 1), :] for q in range(QUARTERS)], axis=1)

    tz = jnp.concatenate([tf[0:8, 0:O], tf[0:8, O:]], axis=0)
    tz_turned = jnp.concatenate([tz[:, O // 2:], tz[:, :O // 2]], axis=1)
    dress = [dot3(split(tz), split(occ_of(0)), NN)]
    oo_swap.wait_recv()
    dress.append(dot3(split(tz_turned), split(occ_of(1)), NN))

    def through(ct, slab, occ):
        ct = split(ct)
        lv = dot3(ct, slab, NN)
        r = split(dot3(ct, occ, NT))
        rt_re, rt_im = dot3(r, amps_re, NN), dot3(r, amps_im, NN)
        parts = []
        for g in range(0, lv.shape[0], 16):
            re, im = slice(g, g + 8), slice(g + 8, g + 16)
            parts.append((
                lv[re] - (rt_re[re] - rt_im[im]),
                lv[im] - (rt_im[re] + rt_re[im]),
            ))
        return parts

    @pl.when(jnp.logical_not(owner))
    def _():
        for w in range(WIN):
            local(z_in.at[w], z_rcv.at[w]).wait()

    cols = jnp.concatenate(
        [part for h in range(WIN) for part in (z_in[h] - dress[h][0:8], -dress[h][8:16])], axis=0)
    slab = (l_hi[...], l_lo[...])

    def exchange(parts):
        for h in range(WIN):
            re, im = fold(w_vir[h], parts[h])
            om[h, :, 0:V] = -re
            om[h, :, V:2 * V] = -im

    first = copy(om.at[1], om_in, r1_snd, r1_rcv, peer, c)

    @pl.when(jnp.logical_not(owner))
    def _():
        exchange(through(cols, slab, oo_own))
        first.start()

    @pl.when(owner)
    def _():
        local(x_all.at[pl.ds(1, 3)], x_rcv).wait()
        x_tot[core] = x_head[...] + x_all[1] + x_all[2] + x_all[3]
        swap = copy(x_tot.at[core], x_tot.at[core], xs_snd, xs_rcv, peer, c)
        swap.start()
        w_re, w_im = weight(e_vir + by_row(PAIR_NODES, V) - e_win[0])
        turns = [HALF * (g - PAIR_MID) for g in PAIR_NODES]
        t_cos = by_row([math.cos(g) for g in turns], V)
        t_sin = by_row([math.sin(g) for g in turns], V)
        local(x_tot.at[1 - core], xs_rcv).wait()
        parts = through(jnp.concatenate([cols, x_tot[0], x_tot[1]], axis=0), slab, oo_own)
        exchange(parts)
        first.start()
        re, im = fold((w_re * t_cos - w_im * t_sin, w_re * t_sin + w_im * t_cos), parts[WIN])
        om[0, :, 0:V] += 2.0 * re
        om[0, :, V:2 * V] += 2.0 * im
        swap.wait_send()

    first.wait_recv()
    om_pl[plane] = om[0] + om_in[...]

    @pl.loop(PLANE, SLOTS - 1)
    def _(k):
        copy(om_pl.at[plane], om_pl.at[plane], r2_snd, r2_rcv, 2 * mate(k) + core, c).start()

    local(om_pl.at[pl.ds(0, PLANE - 1)], r2_rcv).wait()
    total = om_pl[0]
    for k in range(1, PLANE):
        total = total + om_pl[k]
    om_ln[line] = total
    for k in far_line:
        pair, chol = line_mate(k)
        copy(om_ln.at[line], om_ln.at[line], r3_snd, r3_rcv, pair, chol).start()
    local(om_ln.at[pl.ds(0, LINE - 1)], r3_rcv).wait()
    total = om_ln[0]
    for k in range(1, LINE):
        total = total + om_ln[k]
    om_fin[core] = total
    last = copy(om_fin.at[core], om_fin.at[core], r4_snd, r4_rcv, peer, c)
    last.start()
    last_in = om_fin.at[1 - core]
    local(last_in, r4_rcv).wait()
    for i in range(WIN):
        for r in range(2):
            out[r, i:i + 1, :] = om_fin[i, :, r * V:(r + 1) * V]

    last.wait_send()
    local(om_ln.at[pl.ds(0, LINE - 1)], r3_snd).wait()
    local(om_pl.at[pl.ds(0, PLANE - 1)], r2_snd).wait()
    first.wait_send()
    x_swap.wait_send()
    t_swap.wait_send()
    oo_swap.wait_send()
    local(chunks_in, oa_snd).wait()

    @pl.when(jnp.logical_not(owner))
    def _():
        f_copy.wait_send()
        local(msg.at[pl.ds(0, SLOTS - 1), pl.ds(0, SENT)], t_snd).wait()

    @pl.when(jnp.logical_not(head))
    def _():
        x_copy.wait_send()

    @pl.when(head & jnp.logical_not(owner))
    def _():
        head_copy.wait_send()

    @pl.when(relay)
    def _():
        local(z_held, zh_snd).wait()

    @pl.when(owner)
    def _():
        l_copy.wait_send()
        local(parcel_out.at[pl.ds(1, SLOTS - 1)], oc_snd).wait()
        for w in range(WIN):
            local(z_out.at[w, pl.ds(0, SLOTS - 1)], z_snd.at[w]).wait()


def per_device(chol_ov, chol_oo, amplitudes, eps_occ, eps_vir, fock):
    dma = pltpu.SemaphoreType.DMA

    def f32(*shape):
        return pltpu.VMEM(shape, F32)

    def b16(*shape):
        return pltpu.VMEM(shape, BF16)

    scratch = [
        f32(NQ * VB, LANES), f32(O, NQ), f32(2, 1, V), pltpu.SMEM((1,), F32), f32(V), f32(1, V), dma((6,)),
        f32(O * QUARTERS, LANES), f32(O * QUARTERS, LANES), b16(O, NQ), b16(O, NQ),
        b16(NQ, V), b16(NQ, V), f32(2 * RANK, NQ), f32(PAIR, MSG, LANES),
        f32(SLOTS, 8 + MSG, LANES), f32(8 + MSG, LANES), f32(SLOTS, 1, V), f32(NQ * VB, LANES), b16(NQ, V), b16(NQ, V), f32(WIN, O * QUARTERS, LANES),
        b16(RANK * SLOTS, V), b16(RANK * SLOTS, V), b16(2 * O, V), b16(2 * O, V),
        f32(WIN, SLOTS, RANK, NQ), f32(WIN, RANK, NQ), f32(WIN, 4, RANK, NQ),
        f32(2, RANK, NQ), f32(RANK, NQ), f32(RANK, NQ), f32(8, RANK, NQ), f32(RANK, NQ),
        f32(4, RANK, NQ), f32(2, RANK, NQ),
        f32(WIN, 1, 2 * V), f32(1, 2 * V), f32(PLANE, 1, 2 * V), f32(LINE, 1, 2 * V), f32(WIN, 1, 2 * V),
        dma((WIN,)), dma((WIN,)), dma((WIN,)),
    ] + [dma] * 31
    hbm = pl.BlockSpec(memory_space=pltpu.HBM)
    return pl.pallas_call(
        kernel,
        out_shape=jax.ShapeDtypeStruct((2, WIN, V), F32),
        in_specs=[hbm] * 6,
        out_specs=pl.BlockSpec(memory_space=pltpu.VMEM),
        scratch_shapes=scratch,
        compiler_params=pltpu.CompilerParams(
            collective_id=0, has_side_effects=True, vmem_limit_bytes=63 * 2**20
        ),
    )(
        chol_ov.reshape(NQ * VB, LANES), chol_oo.reshape(NQ, O).T, amplitudes, eps_occ, eps_vir, fock
    )


def solution(mesh):
    return jax.shard_map(
        per_device,
        mesh=mesh,
        in_specs=(
            P("chol", "pair", None),
            P("chol", "pair", None),
            P(None, "pair", None),
            P("pair"),
            P(),
            P("pair", None),
        ),
        out_specs=P(),
        check_vma=False,
    )
```

```python
import jax
import jax.numpy as jnp
from jax import lax
from jax.experimental import pallas as pl
from jax.experimental.pallas import tpu as pltpu
from jax.sharding import PartitionSpec as P

WIN = 2
STEP_TIME = 0.7
PAIR, CHOL = 64, 4
SLOTS = PAIR // 2
PLANE = 16
LINE = 8
V, NQ, O = 768, 512, 64
LANES = 128
VB = V // LANES
SENT, MSG = 2 * VB + 1, 16
PART = NQ * VB // SLOTS
MESH = pl.DeviceIdType.MESH
F32 = jnp.float32


def far_first(v):
    return 2 + v - (v // 2) * (2 * v - 1)


class Place:
    def __init__(self):
        p, c = lax.axis_index("pair"), lax.axis_index("chol")
        self.p, self.c = p, c
        self.core = lax.rem(p, 2)
        self.slot = p // 2
        self.peer = p + 1 - 2 * self.core
        self.z, self.x, self.y = self.slot // PLANE, lax.rem(self.slot // 4, 4), lax.rem(self.slot, 4)
        self.line = 2 * c + self.z

    def mate(self, k):
        z = lax.rem(self.z + 1 - k // PLANE, 2)
        x = lax.rem(self.x + far_first(lax.rem(k // 4, 4)), 4)
        y = lax.rem(self.y + far_first(lax.rem(k, 4)), 4)
        return 2 * (z * PLANE + x * 4 + y) + self.core

    def line_mate(self, k):
        z = lax.rem(self.line + k, LINE)
        return lax.rem(self.p, PAIR // 2) + (PAIR // 2) * lax.rem(z, 2), z // 2


def copy(src, dst, snd, rcv, pair, chol):
    return pltpu.make_async_remote_copy(
        src_ref=src, dst_ref=dst, send_sem=snd, recv_sem=rcv,
        device_id=(pair, chol), device_id_type=MESH,
    )


def local(ref, sem):
    return pltpu.make_async_copy(ref, ref, sem)


def greet(pair, chol):
    pl.semaphore_signal(
        pltpu.get_barrier_semaphore(), inc=1, device_id=(pair, chol), device_id_type=MESH)


def spread(ov, oo, amps, eocc, slabs, occs, msgs,
           l_snd, l_rcv, lg_snd, lg_rcv, lp_snd, lp_rcv, o_snd, o_rcv, og_snd, og_rcv, op_snd, op_rcv,
           t_snd, t_rcv, tp_snd, tp_rcv):
    at = Place()
    core, slot, c = at.core, at.slot, at.c

    @pl.loop(0, SLOTS - 1)
    def _(k):
        greet(at.mate(k), c)

    greet(at.peer, c)
    rows = [amps[r, :, LANES * b:LANES * (b + 1)] for r in range(2) for b in range(VB)]
    rows += [jnp.full((MSG - 2 * VB, LANES), eocc[0], F32)]
    msgs[slot, core] = jnp.concatenate(rows, axis=0)
    pl.semaphore_wait(pltpu.get_barrier_semaphore(), SLOTS)

    def part(ref, s):
        return ref.at[pl.ds(pl.multiple_of(PART * s, 8), PART)]

    def tile(ref, s):
        return ref.at[pl.ds(pl.multiple_of(8 * (s // 4), 8), 8), pl.ds(pl.multiple_of(LANES * lax.rem(s, 4), LANES), LANES)]

    mine = msgs.at[slot, core, pl.ds(0, SENT)]

    @pl.loop(0, SLOTS - 1)
    def _(k):
        copy(mine, mine, t_snd, t_rcv, at.mate(k), c).start()

    slab, occ = slabs.at[core], occs.at[core]

    @pl.when(slot == 0)
    def _():
        @pl.loop(0, SLOTS - 1)
        def _(k):
            to = at.mate(k)
            copy(tile(oo, to // 2), tile(occ, to // 2), o_snd, o_rcv, to, c).start()
            copy(part(ov, to // 2), part(slab, to // 2), l_snd, l_rcv, to, c).start()

        slabs[core, 0:PART, :] = ov[0:PART, :]
        occs[core, 0:8, 0:LANES] = oo[0:8, 0:LANES]

    @pl.when(slot != 0)
    def _():
        local(tile(occ, slot), o_rcv).wait()
        local(part(slab, slot), l_rcv).wait()

    @pl.loop(0, SLOTS - 1)
    def _(k):
        to = at.mate(k)
        copy(tile(occ, slot), tile(occ, slot), og_snd, og_rcv, to, c).start()
        copy(part(slab, slot), part(slab, slot), lg_snd, lg_rcv, to, c).start()

    local(msgs.at[pl.ds(0, SLOTS - 1), core, pl.ds(0, SENT)], t_rcv).wait()
    t_rows = msgs.at[:, core, pl.ds(0, SENT)]
    t_swap = copy(t_rows, t_rows, tp_snd, tp_rcv, at.peer, c)
    t_swap.start()
    tiles = ov.at[pl.ds(0, 8 * (SLOTS - 1))]
    parts = ov.at[pl.ds(0, PART * (SLOTS - 1))]
    local(tiles, og_rcv).wait()
    o_swap = copy(occ, occ, op_snd, op_rcv, at.peer, c)
    o_swap.start()
    local(parts, lg_rcv).wait()
    l_swap = copy(slab, slab, lp_snd, lp_rcv, at.peer, c)
    l_swap.start()
    local(msgs.at[:, 1 - core, pl.ds(0, SENT)], tp_rcv).wait()
    local(occs.at[1 - core], op_rcv).wait()
    local(slabs.at[1 - core], lp_rcv).wait()
    t_swap.wait_send()
    o_swap.wait_send()
    l_swap.wait_send()
    local(msgs.at[pl.ds(0, SLOTS - 1), core, pl.ds(0, SENT)], t_snd).wait()
    local(tiles, og_snd).wait()
    local(parts, lg_snd).wait()

    @pl.when(slot == 0)
    def _():
        local(tiles, o_snd).wait()
        local(parts, l_snd).wait()


def add_up(om, out, om_in, om_pl, om_ln, om_fin,
           r1_snd, r1_rcv, r2_snd, r2_rcv, r3_snd, r3_rcv, r4_snd, r4_rcv):
    at = Place()
    core, c = at.core, at.c
    plane = lax.rem(at.slot, PLANE)

    @pl.loop(PLANE, SLOTS - 1)
    def _(k):
        greet(at.mate(k), c)

    for k in range(1, LINE):
        greet(*at.line_mate(k))
    greet(at.peer, c)
    pl.semaphore_wait(pltpu.get_barrier_semaphore(), PLANE + LINE - 1)

    first = copy(om.at[1 - core], om_in, r1_snd, r1_rcv, at.peer, c)
    first.start()
    first.wait_recv()
    om_pl[plane] = om[core] + om_in[...]

    @pl.loop(PLANE, SLOTS - 1)
    def _(k):
        copy(om_pl.at[plane], om_pl.at[plane], r2_snd, r2_rcv, at.mate(k), c).start()

    local(om_pl.at[pl.ds(0, PLANE - 1)], r2_rcv).wait()
    total = om_pl[0]
    for k in range(1, PLANE):
        total = total + om_pl[k]
    om_ln[at.line] = total
    for k in (4, 3, 5, 2, 6, 1, 7):
        pair, chol = at.line_mate(k)
        copy(om_ln.at[at.line], om_ln.at[at.line], r3_snd, r3_rcv, pair, chol).start()
    local(om_ln.at[pl.ds(0, LINE - 1)], r3_rcv).wait()
    total = om_ln[0]
    for k in range(1, LINE):
        total = total + om_ln[k]
    om_fin[core] = total
    last = copy(om_fin.at[core], om_fin.at[core], r4_snd, r4_rcv, at.peer, c)
    last.start()
    local(om_fin.at[1 - core], r4_rcv).wait()
    for i in range(WIN):
        for r in range(2):
            out[r, i:i + 1, :] = om_fin[i, :, r * V:(r + 1) * V]
    last.wait_send()
    first.wait_send()
    local(om_ln.at[pl.ds(0, LINE - 1)], r3_snd).wait()
    local(om_pl.at[pl.ds(0, PLANE - 1)], r2_snd).wait()


def per_device(chol_ov, chol_oo, amplitudes, eps_occ, eps_vir, fock):
    hi = lax.Precision.HIGHEST
    dma = pltpu.SemaphoreType.DMA
    vmem = pl.BlockSpec(memory_space=pltpu.VMEM)
    smem = pl.BlockSpec(memory_space=pltpu.SMEM)
    slabs, occs, msgs = pl.pallas_call(
        spread,
        out_shape=(
            jax.ShapeDtypeStruct((WIN, NQ * VB, LANES), F32),
            jax.ShapeDtypeStruct((WIN, O, NQ), F32),
            jax.ShapeDtypeStruct((SLOTS, 2, MSG, LANES), F32),
        ),
        in_specs=[vmem, vmem, vmem, smem],
        out_specs=(vmem, vmem, vmem),
        scratch_shapes=[dma] * 16,
        compiler_params=pltpu.CompilerParams(
            collective_id=0, has_side_effects=True, vmem_limit_bytes=32 * 2**20),
    )(chol_ov.reshape(NQ * VB, LANES), chol_oo.reshape(NQ, O).T, amplitudes, eps_occ)
    msgs = msgs.reshape(PAIR, MSG, LANES)
    amps_re = msgs[:, 0:VB].reshape(O, V)
    amps_im = msgs[:, VB:2 * VB].reshape(O, V)
    e_win = msgs[0:WIN, 2 * VB, 0]

    def dressed(slab, occ):
        return (slab - jnp.dot(occ, amps_re, precision=hi), -jnp.dot(occ, amps_im, precision=hi))

    right = dressed(chol_ov.reshape(NQ, V), chol_oo.reshape(NQ, O))
    f_row = fock.reshape(1, V)
    f_col = fock.reshape(V, 1)
    y = STEP_TIME * (eps_vir - eps_occ[0])
    cos_y, sin_y = jnp.cos(y)[None, :], jnp.sin(y)[None, :]
    terms = []
    for i in range(WIN):
        left = dressed(slabs[i].reshape(NQ, V), occs[i].T)
        g_re = jnp.dot(left[0].T, right[0], precision=hi) - jnp.dot(left[1].T, right[1], precision=hi)
        g_im = jnp.dot(left[0].T, right[1], precision=hi) + jnp.dot(left[1].T, right[0], precision=hi)
        x = STEP_TIME * (eps_vir - e_win[i])
        cos_x, sin_x = jnp.cos(x)[:, None], jnp.sin(x)[:, None]
        inv = 1.0 / (eps_vir[:, None] + eps_vir[None, :] - e_win[i] - eps_occ[0])
        w_re = (1.0 - (cos_x * cos_y - sin_x * sin_y)) * inv
        w_im = (sin_x * cos_y + cos_x * sin_y) * inv
        t_re = w_re * g_re - w_im * g_im
        t_im = w_re * g_im + w_im * g_re
        o_re = 2.0 * jnp.sum(t_re * f_row, axis=1) - jnp.sum(t_re * f_col, axis=0)
        o_im = 2.0 * jnp.sum(t_im * f_row, axis=1) - jnp.sum(t_im * f_col, axis=0)
        terms.append(jnp.concatenate([o_re, o_im]).reshape(1, 2 * V))
    row = pltpu.VMEM((1, 2 * V), F32)
    return pl.pallas_call(
        add_up,
        out_shape=jax.ShapeDtypeStruct((2, WIN, V), F32),
        in_specs=[vmem],
        out_specs=vmem,
        scratch_shapes=[
            row, pltpu.VMEM((PLANE, 1, 2 * V), F32), pltpu.VMEM((LINE, 1, 2 * V), F32),
            pltpu.VMEM((WIN, 1, 2 * V), F32),
        ] + [dma] * 8,
        compiler_params=pltpu.CompilerParams(collective_id=1, has_side_effects=True),
    )(jnp.stack(terms))


def solution(mesh):
    return jax.shard_map(
        per_device,
        mesh=mesh,
        in_specs=(
            P("chol", "pair", None),
            P("chol", "pair", None),
            P(None, "pair", None),
            P("pair"),
            P(),
            P("pair", None),
        ),
        out_specs=P(),
        check_vma=False,
    )
```

```python
import jax
import jax.numpy as jnp
from jax import lax
from jax.experimental import pallas as pl
from jax.experimental.pallas import tpu as pltpu
from jax.sharding import PartitionSpec as P

WIN = 2
STEP_TIME = 0.7
PAIR, CHOL = 64, 4
SLOTS = PAIR // 2
PLANE = 16
LINE = 8
V, NQ, O = 768, 512, 64
LANES = 128
VB = V // LANES
SENT, MSG = 2 * VB + 1, 16
PART = NQ * VB // SLOTS
MESH = pl.DeviceIdType.MESH
F32 = jnp.float32


def far_first(v):
    return 2 + v - (v // 2) * (2 * v - 1)


class Place:
    def __init__(self):
        p, c = lax.axis_index("pair"), lax.axis_index("chol")
        self.p, self.c = p, c
        self.core = lax.rem(p, 2)
        self.slot = p // 2
        self.peer = p + 1 - 2 * self.core
        self.z, self.x, self.y = self.slot // PLANE, lax.rem(self.slot // 4, 4), lax.rem(self.slot, 4)
        self.line = 2 * c + self.z

    def mate(self, k):
        z = lax.rem(self.z + 1 - k // PLANE, 2)
        x = lax.rem(self.x + far_first(lax.rem(k // 4, 4)), 4)
        y = lax.rem(self.y + far_first(lax.rem(k, 4)), 4)
        return 2 * (z * PLANE + x * 4 + y) + self.core

    def line_mate(self, k):
        z = lax.rem(self.line + k, LINE)
        return lax.rem(self.p, PAIR // 2) + (PAIR // 2) * lax.rem(z, 2), z // 2


def copy(src, dst, snd, rcv, pair, chol):
    return pltpu.make_async_remote_copy(
        src_ref=src, dst_ref=dst, send_sem=snd, recv_sem=rcv,
        device_id=(pair, chol), device_id_type=MESH,
    )


def local(ref, sem):
    return pltpu.make_async_copy(ref, ref, sem)


def greet(pair, chol):
    pl.semaphore_signal(
        pltpu.get_barrier_semaphore(), inc=1, device_id=(pair, chol), device_id_type=MESH)


def spread(ov, oo, amps, eocc, slabs, occs, msgs,
           l_snd, l_rcv, lg_snd, lg_rcv, lp_snd, lp_rcv, o_snd, o_rcv, og_snd, og_rcv, op_snd, op_rcv,
           t_snd, t_rcv, tp_snd, tp_rcv):
    at = Place()
    core, slot, c = at.core, at.slot, at.c

    @pl.loop(0, SLOTS - 1)
    def _(k):
        greet(at.mate(k), c)

    greet(at.peer, c)
    rows = [amps[r, :, LANES * b:LANES * (b + 1)] for r in range(2) for b in range(VB)]
    rows += [jnp.full((MSG - 2 * VB, LANES), eocc[0], F32)]
    msgs[slot, core] = jnp.concatenate(rows, axis=0)
    pl.semaphore_wait(pltpu.get_barrier_semaphore(), SLOTS)

    def part(ref, s):
        return ref.at[pl.ds(pl.multiple_of(PART * s, 8), PART)]

    def tile(ref, s):
        return ref.at[pl.ds(pl.multiple_of(8 * (s // 4), 8), 8), pl.ds(pl.multiple_of(LANES * lax.rem(s, 4), LANES), LANES)]

    mine = msgs.at[slot, core, pl.ds(0, SENT)]

    @pl.loop(0, SLOTS - 1)
    def _(k):
        copy(mine, mine, t_snd, t_rcv, at.mate(k), c).start()

    slab, occ = slabs.at[core], occs.at[core]

    @pl.when(slot == 0)
    def _():
        @pl.loop(0, SLOTS - 1)
        def _(k):
            to = at.mate(k)
            copy(tile(oo, to // 2), tile(occ, to // 2), o_snd, o_rcv, to, c).start()
            copy(part(ov, to // 2), part(slab, to // 2), l_snd, l_rcv, to, c).start()

        slabs[core, 0:PART, :] = ov[0:PART, :]
        occs[core, 0:8, 0:LANES] = oo[0:8, 0:LANES]

    @pl.when(slot != 0)
    def _():
        local(tile(occ, slot), o_rcv).wait()
        local(part(slab, slot), l_rcv).wait()

    @pl.loop(0, SLOTS - 1)
    def _(k):
        to = at.mate(k)
        copy(tile(occ, slot), tile(occ, slot), og_snd, og_rcv, to, c).start()
        copy(part(slab, slot), part(slab, slot), lg_snd, lg_rcv, to, c).start()

    local(msgs.at[pl.ds(0, SLOTS - 1), core, pl.ds(0, SENT)], t_rcv).wait()
    t_rows = msgs.at[:, core, pl.ds(0, SENT)]
    t_swap = copy(t_rows, t_rows, tp_snd, tp_rcv, at.peer, c)
    t_swap.start()
    tiles = ov.at[pl.ds(0, 8 * (SLOTS - 1))]
    parts = ov.at[pl.ds(0, PART * (SLOTS - 1))]
    local(tiles, og_rcv).wait()
    o_swap = copy(occ, occ, op_snd, op_rcv, at.peer, c)
    o_swap.start()
    local(parts, lg_rcv).wait()
    l_swap = copy(slab, slab, lp_snd, lp_rcv, at.peer, c)
    l_swap.start()
    local(msgs.at[:, 1 - core, pl.ds(0, SENT)], tp_rcv).wait()
    local(occs.at[1 - core], op_rcv).wait()
    local(slabs.at[1 - core], lp_rcv).wait()
    t_swap.wait_send()
    o_swap.wait_send()
    l_swap.wait_send()
    local(msgs.at[pl.ds(0, SLOTS - 1), core, pl.ds(0, SENT)], t_snd).wait()
    local(tiles, og_snd).wait()
    local(parts, lg_snd).wait()

    @pl.when(slot == 0)
    def _():
        local(tiles, o_snd).wait()
        local(parts, l_snd).wait()


def add_up(om, out, om_in, om_pl, om_ln, om_fin,
           r1_snd, r1_rcv, r2_snd, r2_rcv, r3_snd, r3_rcv, r4_snd, r4_rcv):
    at = Place()
    core, c = at.core, at.c
    plane = lax.rem(at.slot, PLANE)

    @pl.loop(PLANE, SLOTS - 1)
    def _(k):
        greet(at.mate(k), c)

    for k in range(1, LINE):
        greet(*at.line_mate(k))
    greet(at.peer, c)
    pl.semaphore_wait(pltpu.get_barrier_semaphore(), PLANE + LINE - 1)

    first = copy(om.at[1 - core], om_in, r1_snd, r1_rcv, at.peer, c)
    first.start()
    first.wait_recv()
    om_pl[plane] = om[core] + om_in[...]

    @pl.loop(PLANE, SLOTS - 1)
    def _(k):
        copy(om_pl.at[plane], om_pl.at[plane], r2_snd, r2_rcv, at.mate(k), c).start()

    local(om_pl.at[pl.ds(0, PLANE - 1)], r2_rcv).wait()
    total = om_pl[0]
    for k in range(1, PLANE):
        total = total + om_pl[k]
    om_ln[at.line] = total
    for k in (4, 3, 5, 2, 6, 1, 7):
        pair, chol = at.line_mate(k)
        copy(om_ln.at[at.line], om_ln.at[at.line], r3_snd, r3_rcv, pair, chol).start()
    local(om_ln.at[pl.ds(0, LINE - 1)], r3_rcv).wait()
    total = om_ln[0]
    for k in range(1, LINE):
        total = total + om_ln[k]
    om_fin[core] = total
    last = copy(om_fin.at[core], om_fin.at[core], r4_snd, r4_rcv, at.peer, c)
    last.start()
    local(om_fin.at[1 - core], r4_rcv).wait()
    for i in range(WIN):
        for r in range(2):
            out[r, i:i + 1, :] = om_fin[i, :, r * V:(r + 1) * V]
    last.wait_send()
    first.wait_send()
    local(om_ln.at[pl.ds(0, LINE - 1)], r3_snd).wait()
    local(om_pl.at[pl.ds(0, PLANE - 1)], r2_snd).wait()


def per_device(chol_ov, chol_oo, amplitudes, eps_occ, eps_vir, fock):
    hi = lax.Precision.HIGHEST
    dma = pltpu.SemaphoreType.DMA
    vmem = pl.BlockSpec(memory_space=pltpu.VMEM)
    smem = pl.BlockSpec(memory_space=pltpu.SMEM)
    slabs, occs, msgs = pl.pallas_call(
        spread,
        out_shape=(
            jax.ShapeDtypeStruct((WIN, NQ * VB, LANES), F32),
            jax.ShapeDtypeStruct((WIN, O, NQ), F32),
            jax.ShapeDtypeStruct((SLOTS, 2, MSG, LANES), F32),
        ),
        in_specs=[vmem, vmem, vmem, smem],
        out_specs=(vmem, vmem, vmem),
        scratch_shapes=[dma] * 16,
        compiler_params=pltpu.CompilerParams(
            collective_id=0, has_side_effects=True, vmem_limit_bytes=32 * 2**20),
    )(chol_ov.reshape(NQ * VB, LANES), chol_oo.reshape(NQ, O).T, amplitudes, eps_occ)
    msgs = msgs.reshape(PAIR, MSG, LANES)
    amps_re = msgs[:, 0:VB].reshape(O, V)
    amps_im = msgs[:, VB:2 * VB].reshape(O, V)
    e_win = msgs[0:WIN, 2 * VB, 0]

    def dressed(slab, occ):
        return (slab - jnp.dot(occ, amps_re, precision=hi), -jnp.dot(occ, amps_im, precision=hi))

    right = dressed(chol_ov.reshape(NQ, V), chol_oo.reshape(NQ, O))
    f_row = fock.reshape(1, V)
    f_col = fock.reshape(V, 1)
    both = jnp.concatenate(right, axis=1)
    y = STEP_TIME * (eps_vir - eps_occ[0])
    cos_y, sin_y = jnp.cos(y)[None, :], jnp.sin(y)[None, :]
    terms = []
    for i in range(WIN):
        left = dressed(slabs[i].reshape(NQ, V), occs[i].T)
        g = lax.dot_general(
            jnp.concatenate(left, axis=1), both, (((0,), (0,)), ((), ())), precision=lax.Precision.HIGH)
        g_re = g[:V, :V] - g[V:, V:]
        g_im = g[:V, V:] + g[V:, :V]
        x = STEP_TIME * (eps_vir - e_win[i])
        cos_x, sin_x = jnp.cos(x)[:, None], jnp.sin(x)[:, None]
        inv = 1.0 / (eps_vir[:, None] + eps_vir[None, :] - e_win[i] - eps_occ[0])
        w_re = (1.0 - (cos_x * cos_y - sin_x * sin_y)) * inv
        w_im = (sin_x * cos_y + cos_x * sin_y) * inv
        t_re = w_re * g_re - w_im * g_im
        t_im = w_re * g_im + w_im * g_re
        o_re = 2.0 * jnp.sum(t_re * f_row, axis=1) - jnp.sum(t_re * f_col, axis=0)
        o_im = 2.0 * jnp.sum(t_im * f_row, axis=1) - jnp.sum(t_im * f_col, axis=0)
        terms.append(jnp.concatenate([o_re, o_im]).reshape(1, 2 * V))
    row = pltpu.VMEM((1, 2 * V), F32)
    return pl.pallas_call(
        add_up,
        out_shape=jax.ShapeDtypeStruct((2, WIN, V), F32),
        in_specs=[vmem],
        out_specs=vmem,
        scratch_shapes=[
            row, pltpu.VMEM((PLANE, 1, 2 * V), F32), pltpu.VMEM((LINE, 1, 2 * V), F32),
            pltpu.VMEM((WIN, 1, 2 * V), F32),
        ] + [dma] * 8,
        compiler_params=pltpu.CompilerParams(collective_id=1, has_side_effects=True),
    )(jnp.stack(terms))


def solution(mesh):
    return jax.shard_map(
        per_device,
        mesh=mesh,
        in_specs=(
            P("chol", "pair", None),
            P("chol", "pair", None),
            P(None, "pair", None),
            P("pair"),
            P(),
            P("pair", None),
        ),
        out_specs=P(),
        check_vma=False,
    )
```

```python
import math

import jax
import jax.numpy as jnp
from jax import lax
from jax.experimental import pallas as pl
from jax.experimental.pallas import tpu as pltpu
from jax.sharding import PartitionSpec as P

WIN = 2
STEP_TIME = 0.7
HALF = STEP_TIME / 2
RANK = 8
VIR_LOW, VIR_HIGH = 0.3, 3.0
OCC_LOW, OCC_HIGH = -2.5, -0.4
PAIR, CHOL = 64, 4
SLOTS = PAIR // 2
PLANE = 16
LINE = 8
V, NQ, O = 768, 512, 64
LANES = 128
VB = V // LANES
QUARTERS = NQ // LANES
UNIT = LANES * VB
EPS_AT, SENT, MSG = 2 * VB, 2 * VB + 1, 16
MESH = pl.DeviceIdType.MESH
F32 = jnp.float32
BF16 = jnp.bfloat16
NN = (((1,), (0,)), ((), ()))
NT = (((1,), (1,)), ((), ()))


def nodes_on(low, high):
    mid, half = (low + high) / 2, (high - low) / 2
    return [mid + half * math.cos((2 * m + 1) * math.pi / (2 * RANK)) for m in range(RANK)]


VIR_NODES = nodes_on(VIR_LOW, VIR_HIGH)
PAIR_NODES = nodes_on(VIR_LOW - OCC_HIGH, VIR_HIGH - OCC_LOW)
PAIR_MID = (VIR_LOW - OCC_HIGH + VIR_HIGH - OCC_LOW) / 2


def by_row(values, width):
    row = lax.broadcasted_iota(jnp.int32, (RANK, width), 0)
    out = jnp.full((RANK, width), values[0], F32)
    for m in range(1, RANK):
        out = jnp.where(row == m, F32(values[m]), out)
    return out


def basis(nodes, at):
    scale = []
    for m in range(RANK):
        den = 1.0
        for n in range(RANK):
            if n != m:
                den *= nodes[m] - nodes[n]
        scale.append(1.0 / den)
    width = at.shape[1]
    row = lax.broadcasted_iota(jnp.int32, (RANK, width), 0)
    out = by_row(scale, width)
    for n in range(RANK):
        out = out * jnp.where(row == n, F32(1.0), at - F32(nodes[n]))
    return out


def weight(denom):
    s, c = jnp.sin(HALF * denom), jnp.cos(HALF * denom)
    q = 2.0 * s / denom
    return q * s, q * c


def fold(w, v):
    re = jnp.sum(w[0] * v[0] - w[1] * v[1], axis=0, keepdims=True)
    im = jnp.sum(w[0] * v[1] + w[1] * v[0], axis=0, keepdims=True)
    return re, im


def split(x):
    hi = x.astype(BF16)
    return hi, (x - hi.astype(F32)).astype(BF16)


def dot(a, b, dims):
    return lax.dot_general(a, b, dims, preferred_element_type=F32)


def dot3(a, b, dims):
    a_hi, a_lo = a
    b_hi, b_lo = b
    rows = a_hi.shape[0]
    both = dot(jnp.concatenate([a_hi, a_lo], axis=0), b_hi, dims)
    return both[:rows] + both[rows:] + dot(a_hi, b_lo, dims)


RING = (0, 1, 2, 1)
DIRECT = sorted(
    (at for at in range(1, SLOTS) if at < PLANE or at % 2 == 0),
    key=lambda at: -(at // PLANE + RING[at // 4 % 4] + RING[at % 4]),
)


def held_at(at):
    return at if at < PLANE else PLANE + 4 * (at % 4) + (at - PLANE) // 4


def far_first(v):
    return 2 + v - (v // 2) * (2 * v - 1)


def kernel(
    ov, oo, amps, eocc, evir, fock, out,
    raw, oo_in, amps_in, e_in, ev_in, f_in, in_sem,
    oo_q, oo_p, oo_hi, oo_lo, l_hi, l_lo, x_left, msg,
    parcel_out, parcel, f_rows, l_other, lx_hi, lx_lo, oo_g, fm_hi, fm_lo, rhs_hi, rhs_lo, z_out, z_in, z_held,
    x_out, x_in, x_sum, x_row, x_head, x_all, x_tot, om, om_in, om_pl, om_ln, om_fin,
    z_snd, z_rcv, zh_rcv, zh_snd, xr_rcv, xh_snd, l_snd, l_rcv, f_snd, f_rcv, x_snd, x_rcv, xs_snd, xs_rcv, t_snd, t_rcv, tp_snd, tp_rcv,
    oc_snd, oc_rcv, oa_snd, oa_rcv, op_snd, op_rcv, xp_snd, xp_rcv, r1_snd, r1_rcv, r2_snd, r2_rcv, r3_snd, r3_rcv, r4_snd, r4_rcv,
):
    p, c = lax.axis_index("pair"), lax.axis_index("chol")
    core = lax.rem(p, 2)
    slot = p // 2
    peer = p + 1 - 2 * core
    z_lo, x_at, y_at = slot // PLANE, lax.rem(slot // 4, 4), lax.rem(slot, 4)
    plane = lax.rem(slot, PLANE)
    line = 2 * c + z_lo

    def copy(src, dst, snd, rcv, pair, chol):
        return pltpu.make_async_remote_copy(
            src_ref=src, dst_ref=dst, send_sem=snd, recv_sem=rcv,
            device_id=(pair, chol), device_id_type=MESH,
        )

    def local(ref, sem):
        return pltpu.make_async_copy(ref, ref, sem)

    def mate(k):
        z = lax.rem(z_lo + 1 - k // PLANE, 2)
        x = lax.rem(x_at + far_first(lax.rem(k // 4, 4)), 4)
        y = lax.rem(y_at + far_first(lax.rem(k, 4)), 4)
        return z * PLANE + x * 4 + y

    def line_mate(k):
        z = lax.rem(line + k, LINE)
        return lax.rem(p, PAIR // 2) + (PAIR // 2) * lax.rem(z, 2), z // 2

    far_line = (4, 3, 5, 2, 6, 1, 7)
    owner = slot == 0
    head = slot < 4
    relay = (slot == 1) | (slot == 3)

    inputs = [
        pltpu.make_async_copy(src, dst, in_sem.at[i])
        for i, (src, dst) in enumerate(
            ((amps, amps_in), (fock, f_in), (eocc, e_in), (evir, ev_in), (oo, oo_in), (ov, raw))
        )
    ]
    for cp in inputs:
        cp.start()

    barrier = pltpu.get_barrier_semaphore()

    def greet(pair, chol):
        pl.semaphore_signal(barrier, inc=1, device_id=(pair, chol), device_id_type=MESH)

    @pl.loop(0, SLOTS - 1)
    def _(k):
        greet(2 * mate(k) + core, c)

    greet(peer, c)

    for k in far_line:
        @pl.when(lax.rem(line + k, LINE) // 2 != c)
        def _(k=k):
            greet(*line_mate(k))

    for cp in inputs[:3]:
        cp.wait()
    e_own = e_in[0]
    rows = [amps_in[r, :, LANES * b:LANES * (b + 1)] for r in range(2) for b in range(VB)]
    rows += [jnp.full((MSG - 2 * VB, LANES), e_own, F32)]
    msg[slot] = jnp.concatenate(rows, axis=0)
    flat = msg.reshape(PAIR * MSG, LANES)

    inputs[3].wait()
    e_vir = ev_in[...].reshape(1, V)
    f_row = f_in[...]
    poly = basis(VIR_NODES, jnp.broadcast_to(e_vir, (RANK, V)))
    gap = jnp.broadcast_to(e_vir - e_own, (RANK, V))
    turn = HALF * (gap - PAIR_MID)
    pair_poly = basis(PAIR_NODES, gap) * f_row
    f_pair = jnp.concatenate([pair_poly * jnp.cos(turn), -pair_poly * jnp.sin(turn)], axis=0)
    f_all = split(jnp.concatenate([poly * f_row, f_pair], axis=0))
    f_pair = split(f_pair)

    inputs[4].wait()
    for q in range(QUARTERS):
        oo_q[O * q:O * (q + 1), :] = oo_in[:, LANES * q:LANES * (q + 1)]
    for q in range(QUARTERS):
        at = O * q
        oo_p[at:at + 32, :] = oo_q[pl.ds(at + core, 32, stride=2), :]
        oo_p[at + 32:at + 64, :] = oo_q[pl.ds(at + 1 - core, 32, stride=2), :]
        hi, lo = split(oo_p[at:at + O, :])
        oo_hi[:, LANES * q:LANES * (q + 1)] = hi
        oo_lo[:, LANES * q:LANES * (q + 1)] = lo

    @pl.when(owner)
    def _():
        for to in range(1, SLOTS):
            at = O * (to % 4) + 8 * (to // 4)
            parcel_out[to, 0:8] = oo_p[at:at + 8, :]
            parcel_out[to, 8:8 + MSG] = msg[0]

    inputs[5].wait()
    for b in range(VB):
        hi, lo = split(raw[pl.ds(b, NQ, stride=VB), :])
        l_hi[:, LANES * b:LANES * (b + 1)] = hi
        l_lo[:, LANES * b:LANES * (b + 1)] = lo
    x_left[...] = dot3(f_pair, (l_hi[...], l_lo[...]), NT)

    pl.semaphore_wait(
        barrier,
        1 + (SLOTS - 1) + (LINE - 2),
    )

    f_copy = copy(f_in, f_rows.at[slot], f_snd, f_rcv, core, c)
    l_copy = copy(raw, l_other, l_snd, l_rcv, peer, c)

    @pl.when(jnp.logical_not(owner))
    def _():
        f_copy.start()

    @pl.when(owner)
    def _():
        l_copy.start()
        f_rows[0] = f_in[...]

    @pl.when(jnp.logical_not(owner))
    def _():
        @pl.loop(0, SLOTS - 1)
        def _(k):
            mine = msg.at[slot, pl.ds(0, SENT)]
            copy(mine, mine, t_snd, t_rcv, 2 * mate(k) + core, c).start()

    def pass_on(mine, into):
        @pl.loop(0, SLOTS - 1)
        def _(k):
            copy(mine, into, oa_snd, oa_rcv, 2 * mate(k) + core, c).start()

    oo_own_w = oo_g.at[0]

    def own_chunk(at):
        return oo_own_w.at[pl.ds(at, 8)]

    @pl.when(owner)
    def _():
        for to in sorted(range(1, SLOTS), key=lambda at: -(at // PLANE + RING[at // 4 % 4] + RING[at % 4])):
            copy(parcel_out.at[to], parcel, oc_snd, oc_rcv, 2 * to + core, c).start()

        oo_g[0, 0:8, :] = oo_p[0:8, :]
        pass_on(own_chunk(0), own_chunk(0))

    half = MSG * SLOTS
    chunks_in = oo_p.at[pl.ds(0, 8 * (SLOTS - 1))]
    @pl.when(jnp.logical_not(owner))
    def _():
        local(msg.at[pl.ds(0, SLOTS - 2), pl.ds(0, SENT)], t_rcv).wait()
        local(parcel, oc_rcv).wait()
        msg[0] = parcel[8:8 + MSG]

    t_swap = copy(msg.at[pl.ds(0, SLOTS), pl.ds(0, SENT)], msg.at[pl.ds(SLOTS, SLOTS), pl.ds(0, SENT)],
                  tp_snd, tp_rcv, peer, c)

    @pl.when(jnp.logical_not(owner))
    def _():
        t_swap.start()

    def take_amps(h):
        for r in range(2):
            for b in range(VB):
                hi, lo = split(flat[pl.ds(half * h + VB * r + b, SLOTS, stride=MSG), :])
                at = slice(O * r + SLOTS * h, O * r + SLOTS * (h + 1))
                rhs_hi[at, LANES * b:LANES * (b + 1)] = hi
                rhs_lo[at, LANES * b:LANES * (b + 1)] = lo

    @pl.when(jnp.logical_not(owner))
    def _():
        at = pl.multiple_of(O * lax.rem(slot, 4) + 8 * (slot // 4), 8)
        oo_g[0, pl.ds(at, 8), :] = parcel[0:8]
        pass_on(parcel.at[pl.ds(0, 8)], own_chunk(at))

    def project(w, slab):
        z = dot3((fm_hi[...], fm_lo[...]), slab, NT)
        for s in range(SLOTS):
            z_out[w, held_at(s)] = z[RANK * s:RANK * (s + 1)]
        for y in (1, 3):
            block = z_out.at[w, pl.ds(PLANE + 4 * y, 4)]
            copy(block, z_held.at[w], z_snd.at[w], zh_rcv.at[w], 2 * y + core, c).start()
        for to in DIRECT:
            copy(z_out.at[w, held_at(to)], z_in.at[w], z_snd.at[w], z_rcv.at[w], 2 * to + core, c).start()
        z_in[w] = z_out[w, 0]

    @pl.when(owner)
    def _():
        l_copy.wait_recv()
        for b in range(VB):
            hi, lo = split(l_other[pl.ds(b, NQ, stride=VB), :])
            lx_hi[:, LANES * b:LANES * (b + 1)] = hi
            lx_lo[:, LANES * b:LANES * (b + 1)] = lo
        local(f_rows.at[pl.ds(1, SLOTS - 1)], f_rcv).wait()
        for s in range(0, SLOTS, 2):
            at = slice(RANK * s, RANK * (s + 2))
            hi, lo = split(jnp.concatenate([poly * f_rows[s], poly * f_rows[s + 1]], axis=0))
            fm_hi[at, :] = hi
            fm_lo[at, :] = lo
        project(0, (l_hi[...], l_lo[...]))
        local(msg.at[pl.ds(0, SLOTS - 1), pl.ds(0, SENT)], t_rcv).wait()
        t_swap.start()
        project(1, (lx_hi[...], lx_lo[...]))

    take_amps(0)
    t_swap.wait_recv()
    take_amps(1)

    amps_re = (rhs_hi[0:O, :], rhs_lo[0:O, :])
    amps_im = (rhs_hi[O:2 * O, :], rhs_lo[O:2 * O, :])
    tf = dot3(f_all, (rhs_hi[...], rhs_lo[...]), NT)
    tx = jnp.concatenate([tf[8:16, 0:O] - tf[16:24, O:], tf[8:16, O:] + tf[16:24, 0:O]], axis=0)
    oo_own = (oo_hi[...], oo_lo[...])
    x_terms = x_left[...] - dot3(split(tx), oo_own, NN)
    x_out[0] = x_terms[0:RANK]
    x_out[1] = x_terms[RANK:]
    x_swap = copy(x_out.at[1 - core], x_in, xp_snd, xp_rcv, peer, c)
    x_swap.start()

    e_win = [flat[half * h + EPS_AT:half * h + EPS_AT + 1, 0:1] for h in range(WIN)]
    vir_rows = e_vir + by_row(VIR_NODES, V)
    w_vir = [weight(vir_rows - (e_win[h] + e_own)) for h in range(WIN)]

    @pl.when(relay)
    def _():
        for w in (0,):
            local(z_held.at[w], zh_rcv.at[w]).wait()
            for x in range(4):
                copy(z_held.at[w, x], z_in.at[w], zh_snd, z_rcv.at[w], 2 * (PLANE + 4 * x) + p, c).start()

    x_swap.wait_recv()
    x_sum[...] = x_out[core] + x_in[...]
    x_copy = copy(x_sum, x_row.at[slot // 4], x_snd, xr_rcv, 2 * y_at + core, c)
    head_copy = copy(x_head, x_all.at[slot], xh_snd, x_rcv, core, c)

    @pl.when(jnp.logical_not(head))
    def _():
        x_copy.start()

    @pl.when(relay)
    def _():
        for w in (1,):
            local(z_held.at[w], zh_rcv.at[w]).wait()
            for x in range(4):
                copy(z_held.at[w, x], z_in.at[w], zh_snd, z_rcv.at[w], 2 * (PLANE + 4 * x) + p, c).start()

    @pl.when(head)
    def _():
        local(x_row.at[pl.ds(1, 7)], xr_rcv).wait()
        total = x_sum[...]
        for k in range(1, 8):
            total = total + x_row[k]
        x_head[...] = total

        @pl.when(jnp.logical_not(owner))
        def _():
            head_copy.start()

    local(chunks_in, oa_rcv).wait()
    oo_swap = copy(oo_g.at[0], oo_g.at[1], op_snd, op_rcv, peer, c)
    oo_swap.start()

    def occ_of(h):
        return jnp.concatenate([oo_g[h, O * q:O * (q + 1), :] for q in range(QUARTERS)], axis=1)

    tz = jnp.concatenate([tf[0:8, 0:O], tf[0:8, O:]], axis=0)
    tz_turned = jnp.concatenate([tz[:, O // 2:], tz[:, :O // 2]], axis=1)
    dress = [dot3(split(tz), split(occ_of(0)), NN)]
    oo_swap.wait_recv()
    dress.append(dot3(split(tz_turned), split(occ_of(1)), NN))

    def through(ct, slab, occ):
        ct = split(ct)
        lv = dot3(ct, slab, NN)
        r = split(dot3(ct, occ, NT))
        rt_re, rt_im = dot3(r, amps_re, NN), dot3(r, amps_im, NN)
        parts = []
        for g in range(0, lv.shape[0], 16):
            re, im = slice(g, g + 8), slice(g + 8, g + 16)
            parts.append((
                lv[re] - (rt_re[re] - rt_im[im]),
                lv[im] - (rt_im[re] + rt_re[im]),
            ))
        return parts

    @pl.when(jnp.logical_not(owner))
    def _():
        for w in range(WIN):
            local(z_in.at[w], z_rcv.at[w]).wait()

    cols = jnp.concatenate(
        [part for h in range(WIN) for part in (z_in[h] - dress[h][0:8], -dress[h][8:16])], axis=0)
    slab = (l_hi[...], l_lo[...])

    first = copy(om.at[1], om_in, r1_snd, r1_rcv, peer, c)

    def exchange(parts):
        for h in (1, 0):
            re, im = fold(w_vir[h], parts[h])
            om[h, :, 0:V] = -re
            om[h, :, V:2 * V] = -im
            if h:
                first.start()

    @pl.when(jnp.logical_not(owner))
    def _():
        exchange(through(cols, slab, oo_own))

    @pl.when(owner)
    def _():
        local(x_all.at[pl.ds(1, 3)], x_rcv).wait()
        x_tot[core] = x_head[...] + x_all[1] + x_all[2] + x_all[3]
        swap = copy(x_tot.at[core], x_tot.at[core], xs_snd, xs_rcv, peer, c)
        swap.start()
        w_re, w_im = weight(e_vir + by_row(PAIR_NODES, V) - e_win[0])
        turns = [HALF * (g - PAIR_MID) for g in PAIR_NODES]
        t_cos = by_row([math.cos(g) for g in turns], V)
        t_sin = by_row([math.sin(g) for g in turns], V)
        local(x_tot.at[1 - core], xs_rcv).wait()
        parts = through(jnp.concatenate([cols, x_tot[0], x_tot[1]], axis=0), slab, oo_own)
        exchange(parts)
        re, im = fold((w_re * t_cos - w_im * t_sin, w_re * t_sin + w_im * t_cos), parts[WIN])
        om[0, :, 0:V] += 2.0 * re
        om[0, :, V:2 * V] += 2.0 * im
        swap.wait_send()

    first.wait_recv()
    om_pl[plane] = om[0] + om_in[...]

    @pl.loop(PLANE, SLOTS - 1)
    def _(k):
        copy(om_pl.at[plane], om_pl.at[plane], r2_snd, r2_rcv, 2 * mate(k) + core, c).start()

    local(om_pl.at[pl.ds(0, PLANE - 1)], r2_rcv).wait()
    total = om_pl[0]
    for k in range(1, PLANE):
        total = total + om_pl[k]
    om_ln[line] = total
    for k in far_line:
        pair, chol = line_mate(k)
        copy(om_ln.at[line], om_ln.at[line], r3_snd, r3_rcv, pair, chol).start()
    local(om_ln.at[pl.ds(0, LINE - 1)], r3_rcv).wait()
    total = om_ln[0]
    for k in range(1, LINE):
        total = total + om_ln[k]
    om_fin[core] = total
    last = copy(om_fin.at[core], om_fin.at[core], r4_snd, r4_rcv, peer, c)
    last.start()
    last_in = om_fin.at[1 - core]
    local(last_in, r4_rcv).wait()
    for i in range(WIN):
        for r in range(2):
            out[r, i:i + 1, :] = om_fin[i, :, r * V:(r + 1) * V]

    last.wait_send()
    local(om_ln.at[pl.ds(0, LINE - 1)], r3_snd).wait()
    local(om_pl.at[pl.ds(0, PLANE - 1)], r2_snd).wait()
    first.wait_send()
    x_swap.wait_send()
    t_swap.wait_send()
    oo_swap.wait_send()
    local(chunks_in, oa_snd).wait()

    @pl.when(jnp.logical_not(owner))
    def _():
        f_copy.wait_send()
        local(msg.at[pl.ds(0, SLOTS - 1), pl.ds(0, SENT)], t_snd).wait()

    @pl.when(jnp.logical_not(head))
    def _():
        x_copy.wait_send()

    @pl.when(head & jnp.logical_not(owner))
    def _():
        head_copy.wait_send()

    @pl.when(relay)
    def _():
        local(z_held, zh_snd).wait()

    @pl.when(owner)
    def _():
        l_copy.wait_send()
        local(parcel_out.at[pl.ds(1, SLOTS - 1)], oc_snd).wait()
        for w in range(WIN):
            local(z_out.at[w, pl.ds(0, SLOTS - 1)], z_snd.at[w]).wait()


def per_device(chol_ov, chol_oo, amplitudes, eps_occ, eps_vir, fock):
    dma = pltpu.SemaphoreType.DMA

    def f32(*shape):
        return pltpu.VMEM(shape, F32)

    def b16(*shape):
        return pltpu.VMEM(shape, BF16)

    scratch = [
        f32(NQ * VB, LANES), f32(O, NQ), f32(2, 1, V), pltpu.SMEM((1,), F32), f32(V), f32(1, V), dma((6,)),
        f32(O * QUARTERS, LANES), f32(O * QUARTERS, LANES), b16(O, NQ), b16(O, NQ),
        b16(NQ, V), b16(NQ, V), f32(2 * RANK, NQ), f32(PAIR, MSG, LANES),
        f32(SLOTS, 8 + MSG, LANES), f32(8 + MSG, LANES), f32(SLOTS, 1, V), f32(NQ * VB, LANES), b16(NQ, V), b16(NQ, V), f32(WIN, O * QUARTERS, LANES),
        b16(RANK * SLOTS, V), b16(RANK * SLOTS, V), b16(2 * O, V), b16(2 * O, V),
        f32(WIN, SLOTS, RANK, NQ), f32(WIN, RANK, NQ), f32(WIN, 4, RANK, NQ),
        f32(2, RANK, NQ), f32(RANK, NQ), f32(RANK, NQ), f32(8, RANK, NQ), f32(RANK, NQ),
        f32(4, RANK, NQ), f32(2, RANK, NQ),
        f32(WIN, 1, 2 * V), f32(1, 2 * V), f32(PLANE, 1, 2 * V), f32(LINE, 1, 2 * V), f32(WIN, 1, 2 * V),
        dma((WIN,)), dma((WIN,)), dma((WIN,)),
    ] + [dma] * 31
    hbm = pl.BlockSpec(memory_space=pltpu.HBM)
    return pl.pallas_call(
        kernel,
        out_shape=jax.ShapeDtypeStruct((2, WIN, V), F32),
        in_specs=[hbm] * 6,
        out_specs=pl.BlockSpec(memory_space=pltpu.VMEM),
        scratch_shapes=scratch,
        compiler_params=pltpu.CompilerParams(
            collective_id=0, has_side_effects=True, vmem_limit_bytes=63 * 2**20
        ),
    )(
        chol_ov.reshape(NQ * VB, LANES), chol_oo.reshape(NQ, O).T, amplitudes, eps_occ, eps_vir, fock
    )


def solution(mesh):
    return jax.shard_map(
        per_device,
        mesh=mesh,
        in_specs=(
            P("chol", "pair", None),
            P("chol", "pair", None),
            P(None, "pair", None),
            P("pair"),
            P(),
            P("pair", None),
        ),
        out_specs=P(),
        check_vma=False,
    )
```

```python
import math

import jax
import jax.numpy as jnp
from jax import lax
from jax.experimental import pallas as pl
from jax.experimental.pallas import tpu as pltpu
from jax.sharding import PartitionSpec as P

WIN = 2
STEP_TIME = 0.7
HALF = STEP_TIME / 2
RANK = 8
VIR_LOW, VIR_HIGH = 0.3, 3.0
OCC_LOW, OCC_HIGH = -2.5, -0.4
PAIR, CHOL = 64, 4
SLOTS = PAIR // 2
PLANE = 16
LINE = 8
V, NQ, O = 768, 512, 64
LANES = 128
VB = V // LANES
QUARTERS = NQ // LANES
UNIT = LANES * VB
EPS_AT, SENT, MSG = 2 * VB, 2 * VB + 1, 16
MESH = pl.DeviceIdType.MESH
F32 = jnp.float32
BF16 = jnp.bfloat16
NN = (((1,), (0,)), ((), ()))
NT = (((1,), (1,)), ((), ()))


def nodes_on(low, high):
    mid, half = (low + high) / 2, (high - low) / 2
    return [mid + half * math.cos((2 * m + 1) * math.pi / (2 * RANK)) for m in range(RANK)]


VIR_NODES = nodes_on(VIR_LOW, VIR_HIGH)
PAIR_NODES = nodes_on(VIR_LOW - OCC_HIGH, VIR_HIGH - OCC_LOW)
PAIR_MID = (VIR_LOW - OCC_HIGH + VIR_HIGH - OCC_LOW) / 2


def by_row(values, width):
    row = lax.broadcasted_iota(jnp.int32, (RANK, width), 0)
    out = jnp.full((RANK, width), values[0], F32)
    for m in range(1, RANK):
        out = jnp.where(row == m, F32(values[m]), out)
    return out


def basis(nodes, at):
    scale = []
    for m in range(RANK):
        den = 1.0
        for n in range(RANK):
            if n != m:
                den *= nodes[m] - nodes[n]
        scale.append(1.0 / den)
    width = at.shape[1]
    row = lax.broadcasted_iota(jnp.int32, (RANK, width), 0)
    out = by_row(scale, width)
    for n in range(RANK):
        out = out * jnp.where(row == n, F32(1.0), at - F32(nodes[n]))
    return out


def weight(denom):
    s, c = jnp.sin(HALF * denom), jnp.cos(HALF * denom)
    q = 2.0 * s / denom
    return q * s, q * c


def fold(w, v):
    re = jnp.sum(w[0] * v[0] - w[1] * v[1], axis=0, keepdims=True)
    im = jnp.sum(w[0] * v[1] + w[1] * v[0], axis=0, keepdims=True)
    return re, im


def split(x):
    hi = x.astype(BF16)
    return hi, (x - hi.astype(F32)).astype(BF16)


def dot(a, b, dims):
    return lax.dot_general(a, b, dims, preferred_element_type=F32)


def dot3(a, b, dims):
    a_hi, a_lo = a
    b_hi, b_lo = b
    rows = a_hi.shape[0]
    both = dot(jnp.concatenate([a_hi, a_lo], axis=0), b_hi, dims)
    return both[:rows] + both[rows:] + dot(a_hi, b_lo, dims)


RING = (0, 1, 2, 1)
DIRECT = sorted(
    (at for at in range(1, SLOTS) if at < PLANE or at % 2 == 0),
    key=lambda at: -(at // PLANE + RING[at // 4 % 4] + RING[at % 4]),
)


def held_at(at):
    return at if at < PLANE else PLANE + 4 * (at % 4) + (at - PLANE) // 4


def far_first(v):
    return 2 + v - (v // 2) * (2 * v - 1)


def kernel(
    ov, oo, amps, eocc, evir, fock, out,
    raw, oo_in, amps_in, e_in, ev_in, f_in, in_sem,
    oo_q, oo_p, oo_hi, oo_lo, l_hi, l_lo, x_left, msg,
    parcel_out, parcel, f_rows, l_other, lx_hi, lx_lo, oo_g, fm_hi, fm_lo, rhs_hi, rhs_lo, z_out, z_in, z_held,
    x_out, x_in, x_sum, x_row, x_head, x_all, x_tot, om, om_in, om_pl, om_ln,
    z_snd, z_rcv, zh_rcv, zh_snd, xr_rcv, xh_snd, l_snd, l_rcv, f_snd, f_rcv, x_snd, x_rcv, xs_snd, xs_rcv, t_snd, t_rcv, tp_snd, tp_rcv,
    oc_snd, oc_rcv, oa_snd, oa_rcv, op_snd, op_rcv, xp_snd, xp_rcv, r1_snd, r1_rcv, r2_snd, r2_rcv, r3_snd, r3_rcv,
):
    p, c = lax.axis_index("pair"), lax.axis_index("chol")
    core = lax.rem(p, 2)
    slot = p // 2
    peer = p + 1 - 2 * core
    z_lo, x_at, y_at = slot // PLANE, lax.rem(slot // 4, 4), lax.rem(slot, 4)
    plane = lax.rem(slot, PLANE)
    line = 2 * c + z_lo

    def copy(src, dst, snd, rcv, pair, chol):
        return pltpu.make_async_remote_copy(
            src_ref=src, dst_ref=dst, send_sem=snd, recv_sem=rcv,
            device_id=(pair, chol), device_id_type=MESH,
        )

    def local(ref, sem):
        return pltpu.make_async_copy(ref, ref, sem)

    def mate(k):
        z = lax.rem(z_lo + 1 - k // PLANE, 2)
        x = lax.rem(x_at + far_first(lax.rem(k // 4, 4)), 4)
        y = lax.rem(y_at + far_first(lax.rem(k, 4)), 4)
        return z * PLANE + x * 4 + y

    def line_mate(k):
        z = lax.rem(line + k, LINE)
        return lax.rem(p, PAIR // 2) + (PAIR // 2) * lax.rem(z, 2), z // 2

    far_line = (4, 3, 5, 2, 6, 1, 7)
    owner = slot == 0
    head = slot < 4
    relay = (slot == 1) | (slot == 3)

    inputs = [
        pltpu.make_async_copy(src, dst, in_sem.at[i])
        for i, (src, dst) in enumerate(
            ((amps, amps_in), (fock, f_in), (eocc, e_in), (evir, ev_in), (oo, oo_in), (ov, raw))
        )
    ]
    for cp in inputs:
        cp.start()

    barrier = pltpu.get_barrier_semaphore()

    def greet(pair, chol):
        pl.semaphore_signal(barrier, inc=1, device_id=(pair, chol), device_id_type=MESH)

    @pl.loop(0, SLOTS - 1)
    def _(k):
        greet(2 * mate(k) + core, c)

    greet(peer, c)
    for k in far_line:
        pair, chol = line_mate(k)
        greet(pair + peer - p, chol)

    for k in far_line:
        @pl.when(lax.rem(line + k, LINE) // 2 != c)
        def _(k=k):
            greet(*line_mate(k))

    for cp in inputs[:3]:
        cp.wait()
    e_own = e_in[0]
    rows = [amps_in[r, :, LANES * b:LANES * (b + 1)] for r in range(2) for b in range(VB)]
    rows += [jnp.full((MSG - 2 * VB, LANES), e_own, F32)]
    msg[slot] = jnp.concatenate(rows, axis=0)
    flat = msg.reshape(PAIR * MSG, LANES)

    inputs[3].wait()
    e_vir = ev_in[...].reshape(1, V)
    f_row = f_in[...]
    poly = basis(VIR_NODES, jnp.broadcast_to(e_vir, (RANK, V)))
    gap = jnp.broadcast_to(e_vir - e_own, (RANK, V))
    turn = HALF * (gap - PAIR_MID)
    pair_poly = basis(PAIR_NODES, gap) * f_row
    f_pair = jnp.concatenate([pair_poly * jnp.cos(turn), -pair_poly * jnp.sin(turn)], axis=0)
    f_all = split(jnp.concatenate([poly * f_row, f_pair], axis=0))
    f_pair = split(f_pair)

    inputs[4].wait()
    for q in range(QUARTERS):
        oo_q[O * q:O * (q + 1), :] = oo_in[:, LANES * q:LANES * (q + 1)]
    for q in range(QUARTERS):
        at = O * q
        oo_p[at:at + 32, :] = oo_q[pl.ds(at + core, 32, stride=2), :]
        oo_p[at + 32:at + 64, :] = oo_q[pl.ds(at + 1 - core, 32, stride=2), :]
        hi, lo = split(oo_p[at:at + O, :])
        oo_hi[:, LANES * q:LANES * (q + 1)] = hi
        oo_lo[:, LANES * q:LANES * (q + 1)] = lo

    @pl.when(owner)
    def _():
        for to in range(1, SLOTS):
            at = O * (to % 4) + 8 * (to // 4)
            parcel_out[to, 0:8] = oo_p[at:at + 8, :]
            parcel_out[to, 8:8 + MSG] = msg[0]

    inputs[5].wait()
    for b in range(VB):
        hi, lo = split(raw[pl.ds(b, NQ, stride=VB), :])
        l_hi[:, LANES * b:LANES * (b + 1)] = hi
        l_lo[:, LANES * b:LANES * (b + 1)] = lo
    x_left[...] = dot3(f_pair, (l_hi[...], l_lo[...]), NT)

    pl.semaphore_wait(
        barrier,
        1 + (SLOTS - 1) + (LINE - 2) + (LINE - 1),
    )

    f_copy = copy(f_in, f_rows.at[slot], f_snd, f_rcv, core, c)
    l_copy = copy(raw, l_other, l_snd, l_rcv, peer, c)

    @pl.when(jnp.logical_not(owner))
    def _():
        f_copy.start()

    @pl.when(owner)
    def _():
        l_copy.start()
        f_rows[0] = f_in[...]

    @pl.when(jnp.logical_not(owner))
    def _():
        @pl.loop(0, SLOTS - 1)
        def _(k):
            mine = msg.at[slot, pl.ds(0, SENT)]
            copy(mine, mine, t_snd, t_rcv, 2 * mate(k) + core, c).start()

    def pass_on(mine, into):
        @pl.loop(0, SLOTS - 1)
        def _(k):
            copy(mine, into, oa_snd, oa_rcv, 2 * mate(k) + core, c).start()

    oo_own_w = oo_g.at[0]

    def own_chunk(at):
        return oo_own_w.at[pl.ds(at, 8)]

    @pl.when(owner)
    def _():
        for to in sorted(range(1, SLOTS), key=lambda at: -(at // PLANE + RING[at // 4 % 4] + RING[at % 4])):
            copy(parcel_out.at[to], parcel, oc_snd, oc_rcv, 2 * to + core, c).start()

        oo_g[0, 0:8, :] = oo_p[0:8, :]
        pass_on(own_chunk(0), own_chunk(0))

    half = MSG * SLOTS
    chunks_in = oo_p.at[pl.ds(0, 8 * (SLOTS - 1))]
    @pl.when(jnp.logical_not(owner))
    def _():
        local(msg.at[pl.ds(0, SLOTS - 2), pl.ds(0, SENT)], t_rcv).wait()
        local(parcel, oc_rcv).wait()
        msg[0] = parcel[8:8 + MSG]

    t_swap = copy(msg.at[pl.ds(0, SLOTS), pl.ds(0, SENT)], msg.at[pl.ds(SLOTS, SLOTS), pl.ds(0, SENT)],
                  tp_snd, tp_rcv, peer, c)

    @pl.when(jnp.logical_not(owner))
    def _():
        t_swap.start()

    def take_amps(h):
        for r in range(2):
            for b in range(VB):
                hi, lo = split(flat[pl.ds(half * h + VB * r + b, SLOTS, stride=MSG), :])
                at = slice(O * r + SLOTS * h, O * r + SLOTS * (h + 1))
                rhs_hi[at, LANES * b:LANES * (b + 1)] = hi
                rhs_lo[at, LANES * b:LANES * (b + 1)] = lo

    @pl.when(jnp.logical_not(owner))
    def _():
        at = pl.multiple_of(O * lax.rem(slot, 4) + 8 * (slot // 4), 8)
        oo_g[0, pl.ds(at, 8), :] = parcel[0:8]
        pass_on(parcel.at[pl.ds(0, 8)], own_chunk(at))

    def project(w, slab):
        z = dot3((fm_hi[...], fm_lo[...]), slab, NT)
        for s in range(SLOTS):
            z_out[w, held_at(s)] = z[RANK * s:RANK * (s + 1)]
        for y in (1, 3):
            block = z_out.at[w, pl.ds(PLANE + 4 * y, 4)]
            copy(block, z_held.at[w], z_snd.at[w], zh_rcv.at[w], 2 * y + core, c).start()
        for to in DIRECT:
            copy(z_out.at[w, held_at(to)], z_in.at[w], z_snd.at[w], z_rcv.at[w], 2 * to + core, c).start()
        z_in[w] = z_out[w, 0]

    @pl.when(owner)
    def _():
        l_copy.wait_recv()
        for b in range(VB):
            hi, lo = split(l_other[pl.ds(b, NQ, stride=VB), :])
            lx_hi[:, LANES * b:LANES * (b + 1)] = hi
            lx_lo[:, LANES * b:LANES * (b + 1)] = lo
        local(f_rows.at[pl.ds(1, SLOTS - 1)], f_rcv).wait()
        for s in range(0, SLOTS, 2):
            at = slice(RANK * s, RANK * (s + 2))
            hi, lo = split(jnp.concatenate([poly * f_rows[s], poly * f_rows[s + 1]], axis=0))
            fm_hi[at, :] = hi
            fm_lo[at, :] = lo
        project(0, (l_hi[...], l_lo[...]))
        local(msg.at[pl.ds(0, SLOTS - 1), pl.ds(0, SENT)], t_rcv).wait()
        t_swap.start()
        project(1, (lx_hi[...], lx_lo[...]))

    take_amps(0)
    t_swap.wait_recv()
    take_amps(1)

    amps_re = (rhs_hi[0:O, :], rhs_lo[0:O, :])
    amps_im = (rhs_hi[O:2 * O, :], rhs_lo[O:2 * O, :])
    tf = dot3(f_all, (rhs_hi[...], rhs_lo[...]), NT)
    tx = jnp.concatenate([tf[8:16, 0:O] - tf[16:24, O:], tf[8:16, O:] + tf[16:24, 0:O]], axis=0)
    oo_own = (oo_hi[...], oo_lo[...])
    x_terms = x_left[...] - dot3(split(tx), oo_own, NN)
    x_out[0] = x_terms[0:RANK]
    x_out[1] = x_terms[RANK:]
    x_swap = copy(x_out.at[1 - core], x_in, xp_snd, xp_rcv, peer, c)
    x_swap.start()

    e_win = [flat[half * h + EPS_AT:half * h + EPS_AT + 1, 0:1] for h in range(WIN)]
    vir_rows = e_vir + by_row(VIR_NODES, V)
    w_vir = [weight(vir_rows - (e_win[h] + e_own)) for h in range(WIN)]

    @pl.when(relay)
    def _():
        for w in (0,):
            local(z_held.at[w], zh_rcv.at[w]).wait()
            for x in range(4):
                copy(z_held.at[w, x], z_in.at[w], zh_snd, z_rcv.at[w], 2 * (PLANE + 4 * x) + p, c).start()

    x_swap.wait_recv()
    x_sum[...] = x_out[core] + x_in[...]
    x_copy = copy(x_sum, x_row.at[slot // 4], x_snd, xr_rcv, 2 * y_at + core, c)
    head_copy = copy(x_head, x_all.at[slot], xh_snd, x_rcv, core, c)

    @pl.when(jnp.logical_not(head))
    def _():
        x_copy.start()

    @pl.when(relay)
    def _():
        for w in (1,):
            local(z_held.at[w], zh_rcv.at[w]).wait()
            for x in range(4):
                copy(z_held.at[w, x], z_in.at[w], zh_snd, z_rcv.at[w], 2 * (PLANE + 4 * x) + p, c).start()

    @pl.when(head)
    def _():
        local(x_row.at[pl.ds(1, 7)], xr_rcv).wait()
        total = x_sum[...]
        for k in range(1, 8):
            total = total + x_row[k]
        x_head[...] = total

        @pl.when(jnp.logical_not(owner))
        def _():
            head_copy.start()

    local(chunks_in, oa_rcv).wait()
    oo_swap = copy(oo_g.at[0], oo_g.at[1], op_snd, op_rcv, peer, c)
    oo_swap.start()

    def occ_of(h):
        return jnp.concatenate([oo_g[h, O * q:O * (q + 1), :] for q in range(QUARTERS)], axis=1)

    tz = jnp.concatenate([tf[0:8, 0:O], tf[0:8, O:]], axis=0)
    tz_turned = jnp.concatenate([tz[:, O // 2:], tz[:, :O // 2]], axis=1)
    dress = [dot3(split(tz), split(occ_of(0)), NN)]
    oo_swap.wait_recv()
    dress.append(dot3(split(tz_turned), split(occ_of(1)), NN))

    def through(ct, slab, occ):
        ct = split(ct)
        lv = dot3(ct, slab, NN)
        r = split(dot3(ct, occ, NT))
        rt_re, rt_im = dot3(r, amps_re, NN), dot3(r, amps_im, NN)
        parts = []
        for g in range(0, lv.shape[0], 16):
            re, im = slice(g, g + 8), slice(g + 8, g + 16)
            parts.append((
                lv[re] - (rt_re[re] - rt_im[im]),
                lv[im] - (rt_im[re] + rt_re[im]),
            ))
        return parts

    @pl.when(jnp.logical_not(owner))
    def _():
        for w in range(WIN):
            local(z_in.at[w], z_rcv.at[w]).wait()

    cols = jnp.concatenate(
        [part for h in range(WIN) for part in (z_in[h] - dress[h][0:8], -dress[h][8:16])], axis=0)
    slab = (l_hi[...], l_lo[...])

    first = copy(om.at[1], om_in, r1_snd, r1_rcv, peer, c)

    def exchange(parts):
        for h in (1, 0):
            re, im = fold(w_vir[h], parts[h])
            om[h, :, 0:V] = -re
            om[h, :, V:2 * V] = -im
            if h:
                first.start()

    @pl.when(jnp.logical_not(owner))
    def _():
        exchange(through(cols, slab, oo_own))

    @pl.when(owner)
    def _():
        local(x_all.at[pl.ds(1, 3)], x_rcv).wait()
        x_tot[core] = x_head[...] + x_all[1] + x_all[2] + x_all[3]
        swap = copy(x_tot.at[core], x_tot.at[core], xs_snd, xs_rcv, peer, c)
        swap.start()
        w_re, w_im = weight(e_vir + by_row(PAIR_NODES, V) - e_win[0])
        turns = [HALF * (g - PAIR_MID) for g in PAIR_NODES]
        t_cos = by_row([math.cos(g) for g in turns], V)
        t_sin = by_row([math.sin(g) for g in turns], V)
        local(x_tot.at[1 - core], xs_rcv).wait()
        parts = through(jnp.concatenate([cols, x_tot[0], x_tot[1]], axis=0), slab, oo_own)
        exchange(parts)
        re, im = fold((w_re * t_cos - w_im * t_sin, w_re * t_sin + w_im * t_cos), parts[WIN])
        om[0, :, 0:V] += 2.0 * re
        om[0, :, V:2 * V] += 2.0 * im
        swap.wait_send()

    first.wait_recv()
    om_pl[plane] = om[0] + om_in[...]

    @pl.loop(PLANE, SLOTS - 1)
    def _(k):
        copy(om_pl.at[plane], om_pl.at[plane], r2_snd, r2_rcv, 2 * mate(k) + core, c).start()

    local(om_pl.at[pl.ds(0, PLANE - 1)], r2_rcv).wait()
    total = om_pl[0]
    for k in range(1, PLANE):
        total = total + om_pl[k]
    om_ln[core, line] = total
    mine = om_ln.at[core, line]
    for k in far_line:
        pair, chol = line_mate(k)
        copy(mine, mine, r3_snd, r3_rcv, pair, chol).start()
        copy(mine, mine, r3_snd, r3_rcv, pair + peer - p, chol).start()
    copy(mine, mine, r3_snd, r3_rcv, peer, c).start()
    lines = om_ln.reshape(2 * LINE, 1, 2 * V).at[pl.ds(0, 2 * LINE - 1)]
    local(lines, r3_rcv).wait()
    for i in range(WIN):
        total = om_ln[i, 0]
        for k in range(1, LINE):
            total = total + om_ln[i, k]
        for r in range(2):
            out[r, i:i + 1, :] = total[:, r * V:(r + 1) * V]

    local(lines, r3_snd).wait()
    local(om_pl.at[pl.ds(0, PLANE - 1)], r2_snd).wait()
    first.wait_send()
    x_swap.wait_send()
    t_swap.wait_send()
    oo_swap.wait_send()
    local(chunks_in, oa_snd).wait()

    @pl.when(jnp.logical_not(owner))
    def _():
        f_copy.wait_send()
        local(msg.at[pl.ds(0, SLOTS - 1), pl.ds(0, SENT)], t_snd).wait()

    @pl.when(jnp.logical_not(head))
    def _():
        x_copy.wait_send()

    @pl.when(head & jnp.logical_not(owner))
    def _():
        head_copy.wait_send()

    @pl.when(relay)
    def _():
        local(z_held, zh_snd).wait()

    @pl.when(owner)
    def _():
        l_copy.wait_send()
        local(parcel_out.at[pl.ds(1, SLOTS - 1)], oc_snd).wait()
        for w in range(WIN):
            local(z_out.at[w, pl.ds(0, SLOTS - 1)], z_snd.at[w]).wait()


def per_device(chol_ov, chol_oo, amplitudes, eps_occ, eps_vir, fock):
    dma = pltpu.SemaphoreType.DMA

    def f32(*shape):
        return pltpu.VMEM(shape, F32)

    def b16(*shape):
        return pltpu.VMEM(shape, BF16)

    scratch = [
        f32(NQ * VB, LANES), f32(O, NQ), f32(2, 1, V), pltpu.SMEM((1,), F32), f32(V), f32(1, V), dma((6,)),
        f32(O * QUARTERS, LANES), f32(O * QUARTERS, LANES), b16(O, NQ), b16(O, NQ),
        b16(NQ, V), b16(NQ, V), f32(2 * RANK, NQ), f32(PAIR, MSG, LANES),
        f32(SLOTS, 8 + MSG, LANES), f32(8 + MSG, LANES), f32(SLOTS, 1, V), f32(NQ * VB, LANES), b16(NQ, V), b16(NQ, V), f32(WIN, O * QUARTERS, LANES),
        b16(RANK * SLOTS, V), b16(RANK * SLOTS, V), b16(2 * O, V), b16(2 * O, V),
        f32(WIN, SLOTS, RANK, NQ), f32(WIN, RANK, NQ), f32(WIN, 4, RANK, NQ),
        f32(2, RANK, NQ), f32(RANK, NQ), f32(RANK, NQ), f32(8, RANK, NQ), f32(RANK, NQ),
        f32(4, RANK, NQ), f32(2, RANK, NQ),
        f32(WIN, 1, 2 * V), f32(1, 2 * V), f32(PLANE, 1, 2 * V), f32(WIN, LINE, 1, 2 * V),
        dma((WIN,)), dma((WIN,)), dma((WIN,)),
    ] + [dma] * 29
    hbm = pl.BlockSpec(memory_space=pltpu.HBM)
    return pl.pallas_call(
        kernel,
        out_shape=jax.ShapeDtypeStruct((2, WIN, V), F32),
        in_specs=[hbm] * 6,
        out_specs=pl.BlockSpec(memory_space=pltpu.VMEM),
        scratch_shapes=scratch,
        compiler_params=pltpu.CompilerParams(
            collective_id=0, has_side_effects=True, vmem_limit_bytes=63 * 2**20
        ),
    )(
        chol_ov.reshape(NQ * VB, LANES), chol_oo.reshape(NQ, O).T, amplitudes, eps_occ, eps_vir, fock
    )


def solution(mesh):
    return jax.shard_map(
        per_device,
        mesh=mesh,
        in_specs=(
            P("chol", "pair", None),
            P("chol", "pair", None),
            P(None, "pair", None),
            P("pair"),
            P(),
            P("pair", None),
        ),
        out_specs=P(),
        check_vma=False,
    )
```
